32 devices in a mesh: grp: 2 (over y), tm: 4 (over z), freq: 4 (over x, core).
Axes of the slice: x: 2, y: 2, z: 4, core: 2. Of those that a mesh axis runs over, the one named last changes fastest.
Arguments:
- visibilities: bfloat16 [2, 132, 64, 1536], P(None, 'grp', 'tm', 'freq'), parts along dimension 1, may hold values from -6 to 6
- class_ids: int32 [132], P('grp'), parts along dimension 0, may hold values from 0 to 3, as said below
- class_counts: int32 [8], P('grp'), parts along dimension 0, may hold values from 1 to 32, as said below
- tap_windows: int32 [8], P('grp'), parts along dimension 0, may hold values from 1 to 4, as said below
- fringe_taps: float32 [2, 8, 9], P(None, 'grp'), parts along dimension 1, may hold values from -2.4 to 2.4
- flag_mask: int32 [64, 1536], P('freq'), may hold values 0 or 1
- filter_panels: bfloat16 [8, 1536, 1536], P(('grp', 'tm'), 'freq'), parts along dimension 0
Outputs:
- cleaned: bfloat16 [2, 8, 32, 64, 1536], P(None, ('grp', 'tm'), None, 'freq'), parts along dimension 1
The draws below stay inside these ranges and needn't reach their ends.
There are 2 independent parts, one for each index of `grp`. The reference program is written for one: setup_inputs(seed, part) draws one part's arguments, and reference() takes and returns one part's arrays. A program takes and returns all parts, laid end to end along the dimension named above; an argument that names none is the same for every part. Nothing has to cross between parts.
Inputs may be any that keep to these rules, and one draw needn't show every extreme that they name: Baselines are listed grouped by class in increasing order of class; class_ids[b] is the class of baseline b. class_counts[c] is the number of baselines whose class is c; some class has exactly 32 baselines. `tap_windows`: some class has a window of exactly 4.
All inputs are finite; a program needn't handle non-finite values. No bound on the sum of `flag_mask` on one device may be relied on, other than what follows from the above.
Results may differ from the reference program's by a relative error of at most 0.0049.
Values may be sent and summed in bfloat16 or wider, within the bound.
A program may use at most 128 MiB of HBM per device.

```python
import jax
import jax.numpy as jnp
from jax import lax

CHANNEL_COUNT = 1536
SLOTS = 32
REACH = 4
CLASSES = 4
BASELINE_COUNT = 66
TIME_STEPS = 64


def class_layout(key):
    first_member = jax.random.randint(jax.random.fold_in(key, 11), (CLASSES // 2,), 1, SLOTS + 1)
    first_member = first_member.at[0].set(SLOTS)
    paired = jnp.stack([first_member, SLOTS + 1 - first_member], axis=1).reshape(-1)
    class_order = jax.random.permutation(jax.random.fold_in(key, 12), CLASSES)
    return paired[class_order].astype(jnp.int32)


def draw_class_counts(key, part):
    return class_layout(key)


def draw_class_ids(key, part):
    class_ends = jnp.cumsum(class_layout(key))
    baseline_positions = jnp.arange(BASELINE_COUNT, dtype=jnp.int32)
    return jnp.sum((baseline_positions[:, None] >= class_ends[None, :]).astype(jnp.int32), axis=1).astype(jnp.int32)


def draw_tap_windows(key, part):
    window_base = jax.random.randint(jax.random.fold_in(key, 21), (CLASSES,), 1, REACH + 1)
    widest = jax.random.randint(jax.random.fold_in(key, 22), (), 0, CLASSES)
    return jnp.where(jnp.arange(CLASSES, dtype=jnp.int32) == widest, REACH, window_base).astype(jnp.int32)


def draw_filter_panels(key, part):
    spread = jax.random.normal(jax.random.fold_in(key, 31), (CLASSES, CHANNEL_COUNT, CHANNEL_COUNT), jnp.float32)
    diagonal_level = jax.random.uniform(jax.random.fold_in(key, 32), (CLASSES, CHANNEL_COUNT), jnp.float32, 0.3, 0.7)
    channel_iota = jnp.arange(CHANNEL_COUNT, dtype=jnp.int32)
    identity_part = (channel_iota[:, None] == channel_iota[None, :]).astype(jnp.float32)
    panels_full = spread * (0.5 / CHANNEL_COUNT ** 0.5) + identity_part[None, :, :] * diagonal_level[:, :, None]
    return panels_full.astype(jnp.bfloat16)


def place_ends(array, own_key, smallest, largest):
    place = [jax.random.randint(jax.random.fold_in(own_key, axis), (), 0, length) for axis, length in enumerate(array.shape)]
    main_axis = array.shape.index(max(array.shape))
    next_to = place[:main_axis] + [(place[main_axis] + 1) % array.shape[main_axis]] + place[main_axis + 1:]
    return array.at[tuple(place)].set(smallest).at[tuple(next_to)].set(largest)


def steps_of(rng, dims, split, smallest, largest):
    gain, own = 1.0, jax.random.fold_in(rng, 6)
    for position, parts in split:
        draws = jnp.exp(jax.random.uniform(jax.random.fold_in(own, position), (parts,), jnp.float32, smallest / len(split), largest / len(split)))
        gain = gain * jnp.repeat(draws, dims[position] // parts).reshape([-1 if axis == position else 1 for axis in range(len(dims))])
    return gain


def noise(stream_key, shape, scale, most, shards=(), kind=jnp.bfloat16):
    entries = jax.random.normal(stream_key, shape, jnp.float32) * scale
    if len(shards) > 0:
        entries = steps_of(stream_key, shape, shards, -0.22, 0.18) * entries
    return jnp.clip(entries, min=-most, max=most).astype(kind)


def setup_inputs(seed: int = 0, part: int = 0) -> dict:
    keys = jax.random.split(jax.random.key(seed), 8)
    part_splits = jax.random.split(jax.random.fold_in(keys[7], part), 8)
    visibilities = noise(part_splits[0], (2, BASELINE_COUNT, TIME_STEPS, CHANNEL_COUNT), 1.0, 6.0, ((2, 4), (3, 4)))
    class_ids = draw_class_ids(jax.random.fold_in(jax.random.fold_in(keys[7], part), 71), part)
    class_counts = draw_class_counts(jax.random.fold_in(jax.random.fold_in(keys[7], part), 71), part)
    tap_windows = draw_tap_windows(jax.random.fold_in(jax.random.fold_in(keys[7], part), 71), part)
    fringe_taps = noise(part_splits[4], (2, CLASSES, 2 * REACH + 1), 0.4, 2.4, (), jnp.float32)
    flag_mask = place_ends((jax.random.randint(keys[5], (TIME_STEPS, CHANNEL_COUNT), 0, 8) < 7).astype(jnp.int32), jax.random.fold_in(keys[5], 1), 0, 1)
    filter_panels = draw_filter_panels(jax.random.fold_in(jax.random.fold_in(keys[7], part), 71), part)
    return dict(visibilities=visibilities, class_ids=class_ids, class_counts=class_counts, tap_windows=tap_windows, fringe_taps=fringe_taps, flag_mask=flag_mask, filter_panels=filter_panels)


def masked_taps(fringe_taps, tap_windows):
    offsets = jnp.abs(jnp.arange(2 * REACH + 1, dtype=jnp.int32) - REACH)
    keep = (offsets[None, :] <= tap_windows[:, None]).astype(jnp.float32)
    return fringe_taps * keep[None, :, :]


def reference(visibilities, class_ids, class_counts, tap_windows, fringe_taps, flag_mask, filter_panels):
    row_taps = masked_taps(fringe_taps, tap_windows)[:, class_ids, :]
    padded = jnp.pad(visibilities.astype(jnp.float32), ((0, 0), (0, 0), (REACH, REACH), (0, 0)))
    real_part = jnp.zeros(visibilities.shape[1:], jnp.float32)
    imag_part = jnp.zeros(visibilities.shape[1:], jnp.float32)
    for offset in range(2 * REACH + 1):
        shifted = padded[:, :, 2 * REACH - offset:2 * REACH - offset + TIME_STEPS, :]
        tap_real = row_taps[0, :, offset][:, None, None]
        tap_imag = row_taps[1, :, offset][:, None, None]
        real_part = real_part + tap_real * shifted[0] - tap_imag * shifted[1]
        imag_part = imag_part + tap_real * shifted[1] + tap_imag * shifted[0]
    filtered = jnp.stack([real_part, imag_part]).astype(jnp.bfloat16)
    class_starts = jnp.cumsum(class_counts) - class_counts
    flag_gate = flag_mask.astype(jnp.bfloat16)
    slot_positions = jnp.arange(SLOTS, dtype=jnp.int32)

    def one_class(class_number_index):
        input_visibility = jnp.clip(class_starts[class_number_index] + slot_positions, 0, BASELINE_COUNT - 1).astype(jnp.int32)
        live_slot = slot_positions < class_counts[class_number_index]
        slot_rows = jnp.take(filtered, input_visibility, axis=1)
        slot_rows = jnp.where(live_slot[None, :, None, None], slot_rows, jnp.zeros((), jnp.bfloat16))
        weighted = slot_rows * flag_gate
        dayenu_fit = jnp.einsum("rstj,ij->rsti", weighted.astype(jnp.float32), filter_panels[class_number_index].astype(jnp.float32))
        return (slot_rows.astype(jnp.float32) - dayenu_fit).astype(jnp.bfloat16)

    cleaned = lax.map(one_class, jnp.arange(CLASSES, dtype=jnp.int32))
    return jnp.moveaxis(cleaned, 0, 1)
```

```python
import functools

import jax
import jax.numpy as jnp
from jax import lax
from jax.experimental import pallas as pl
from jax.experimental.pallas import tpu as pltpu
from jax.sharding import PartitionSpec as P

SLOTS = 32
REACH = 4
CHUNK = 4
MESH = pl.DeviceIdType.MESH


def extended(cells, sides, width):
    for axis, dim in sides:
        count = lax.axis_size(axis)
        ends = count - 1
        head = lax.slice_in_dim(cells, 0, width, axis=dim)
        tail = lax.slice_in_dim(cells, cells.shape[dim] - width, cells.shape[dim], axis=dim)
        cells = jnp.concatenate(
            [
                lax.ppermute(tail, axis, [(i, (i + 1) % count) for i in range(ends)]),
                cells,
                lax.ppermute(head, axis, [((i + 1) % count, i) for i in range(ends)]),
            ],
            axis=dim,
        )
    return cells


def masked_taps(fringe_taps, tap_windows):
    offsets = jnp.abs(jnp.arange(2 * REACH + 1, dtype=jnp.int32) - REACH)
    keep = (offsets[None, :] <= tap_windows[:, None]).astype(jnp.float32)
    return fringe_taps * keep[None, :, :]


def convolve(padded, row_taps, length):
    real_part = jnp.zeros(padded.shape[1:2] + (length,) + padded.shape[3:], jnp.float32)
    imag_part = jnp.zeros_like(real_part)
    for offset in range(2 * REACH + 1):
        shifted = lax.slice_in_dim(padded, 2 * REACH - offset, 2 * REACH - offset + length, axis=2)
        tap_real = row_taps[0, :, offset][:, None, None]
        tap_imag = row_taps[1, :, offset][:, None, None]
        real_part = real_part + tap_real * shifted[0] - tap_imag * shifted[1]
        imag_part = imag_part + tap_real * shifted[1] + tap_imag * shifted[0]
    return jnp.stack([real_part, imag_part]).astype(jnp.bfloat16)


def to_slots(per_baseline, class_counts):
    class_starts = jnp.cumsum(class_counts) - class_counts
    slot_positions = jnp.arange(SLOTS, dtype=jnp.int32)
    input_visibility = jnp.clip(
        class_starts[:, None] + slot_positions[None, :], 0, per_baseline.shape[1] - 1
    )
    live_slot = slot_positions[None, :] < class_counts[:, None]
    gathered = jnp.take(per_baseline, input_visibility.reshape(-1), axis=1)
    gathered = gathered.reshape(per_baseline.shape[:1] + live_slot.shape + per_baseline.shape[2:])
    return jnp.where(live_slot[None, :, :, None, None], gathered, jnp.zeros((), per_baseline.dtype))


def plain_shards(
    visibilities, class_ids, class_counts, tap_windows, fringe_taps, flag_mask, filter_panels
):
    taps_kept = masked_taps(fringe_taps, tap_windows)
    padded = extended(visibilities, (("tm", 2),), REACH)
    class_iota = jnp.arange(taps_kept.shape[1], dtype=jnp.int32)
    one_hot = (class_ids[:, None] == class_iota[None, :]).astype(jnp.float32)
    row_taps = jnp.einsum("bc,rck->rbk", one_hot, taps_kept, precision=lax.Precision.HIGHEST)
    filtered = convolve(padded, row_taps, visibilities.shape[2])
    slotted = to_slots(filtered, class_counts)
    local_block = lax.all_to_all(
        lax.all_to_all(slotted, "tm", split_axis=1, concat_axis=3, tiled=True),
        "freq",
        split_axis=3,
        concat_axis=4,
        tiled=True,
    )
    flag_gate = flag_mask.astype(jnp.bfloat16)
    weighted = local_block * flag_gate
    dayenu_fit = jnp.einsum(
        "rcstj,cij->rcsti",
        weighted,
        lax.all_gather(filter_panels, "freq", axis=1, tiled=True),
        preferred_element_type=jnp.float32,
    )
    return (local_block.astype(jnp.float32) - dayenu_fit).astype(jnp.bfloat16)


def tap_matrix(taps_ref, windows_ref, own_class, steps, block):
    size = 2 * steps
    out_pos = lax.broadcasted_iota(jnp.int32, (size, size), 0)
    in_pos = lax.broadcasted_iota(jnp.int32, (size, size), 1)

    def parts(pos):
        return (pos // (2 * block)) * block + pos % block, (pos // block) % 2

    out_t, out_r = parts(out_pos)
    in_t, in_r = parts(in_pos)
    lag = out_t - in_t
    same = out_r == in_r
    sign = (out_r - in_r).astype(jnp.float32)
    matrix = jnp.zeros((size, size), jnp.float32)
    window = windows_ref[own_class]
    for offset in range(2 * REACH + 1):
        keep = jnp.where(abs(offset - REACH) <= window, 1.0, 0.0)
        real = taps_ref[0, own_class, offset] * keep
        imag = taps_ref[1, own_class, offset] * keep
        value = jnp.where(same, real, sign * imag)
        matrix = jnp.where(lag == offset - REACH, value, matrix)
    return matrix


def kernel(
    groups,
    lanes,
    counts_ref,
    windows_ref,
    taps_ref,
    vis_ref,
    flag_ref,
    panel_ref,
    out_ref,
    send_z,
    land_z,
    send_x,
    land_x,
    panels,
    taps_mat,
    weighted,
    result,
    z_send_sem,
    z_recv_sem,
    x_send_sem,
    x_recv_sem,
    p_send_sem,
    p_recv_sem,
    local_sem,
    out_sem,
):
    my_z = lax.axis_index("tm")
    my_f = lax.axis_index("freq")
    chunks = SLOTS // CHUNK
    block = vis_ref.shape[2]
    width = vis_ref.shape[3]
    baselines = vis_ref.shape[1]
    rows = 2 * CHUNK * block

    def z_peer(d):
        return lax.rem(my_z + d, groups)

    def f_peer(d):
        return lax.rem(my_f + d, lanes)

    core_peer = my_f + 1 - 2 * lax.rem(my_f, 2)
    x_peer = f_peer(2)
    far_peer = core_peer + 2 - 4 * (core_peer // 2)

    barrier = pltpu.get_barrier_semaphore()
    for d in range(1, groups):
        pl.semaphore_signal(barrier, inc=1, device_id={"tm": z_peer(d)}, device_id_type=MESH)
    for d in range(1, lanes):
        pl.semaphore_signal(barrier, inc=1, device_id={"freq": f_peer(d)}, device_id_type=MESH)
    pl.semaphore_wait(barrier, groups + lanes - 2)

    def panel_copy(which, source, owner, target):
        return pltpu.make_async_remote_copy(
            src_ref=source,
            dst_ref=panels.at[owner],
            send_sem=p_send_sem.at[which],
            recv_sem=p_recv_sem.at[which],
            device_id={"freq": target},
            device_id_type=MESH,
        )

    to_x = panel_copy(0, panel_ref.at[0], my_f, x_peer)
    to_core = panel_copy(1, panel_ref.at[0], my_f, core_peer)
    own_panel = pltpu.make_async_copy(panel_ref.at[0], panels.at[my_f], local_sem)

    def z_copy(q, target, source):
        return pltpu.make_async_remote_copy(
            src_ref=send_z.at[q, target],
            dst_ref=land_z.at[q, source],
            send_sem=z_send_sem.at[q, target],
            recv_sem=z_recv_sem.at[q, source],
            device_id={"tm": target},
            device_id_type=MESH,
        )

    def x_copy(q, target, source):
        return pltpu.make_async_remote_copy(
            src_ref=send_x.at[q, target],
            dst_ref=land_x.at[q, source],
            send_sem=x_send_sem.at[q, target],
            recv_sem=x_recv_sem.at[q, source],
            device_id={"freq": target},
            device_id_type=MESH,
        )

    def start_of(number):
        total = 0
        for i in range(groups):
            total = total + jnp.where(i < number, counts_ref[i], 0)
        return total

    starts = [start_of(z_peer(d)) for d in range(groups)]

    def pick(d, q, store):
        for s in range(CHUNK):
            row = jnp.minimum(starts[d] + q * CHUNK + s, baselines - 1)
            for r in range(2):
                store(r, s, vis_ref[r, row])

    def send_chunk(q, carry):
        for d in (2, 1, 3):
            target = z_peer(d)

            def store(r, s, value):
                send_z[q, target, r, s] = value

            pick(d, q, store)
            z_copy(q, target, my_z).start()
        return carry

    send_chunk(0, 0)
    to_x.start()
    to_core.start()
    own_panel.start()
    lax.fori_loop(1, chunks, send_chunk, 0)

    def keep_chunk(q, carry):
        def store(r, s, value):
            land_z[q, my_z, r, s] = value

        pick(0, q, store)
        return carry

    lax.fori_loop(0, chunks, keep_chunk, 0)

    full = tap_matrix(taps_ref, windows_ref, my_z, groups * block, block)
    size = 2 * groups * block
    high = full.astype(jnp.bfloat16)
    taps_mat[:size, :] = high
    taps_mat[size:, :] = (full - high.astype(jnp.float32)).astype(jnp.bfloat16)
    live_count = counts_ref[my_z]

    def filter_chunk(q, carry):
        for d in range(1, groups):
            z_copy(q, my_z, z_peer(d)).wait_recv()
        for s in range(CHUNK):
            cells = land_z[q, :, :, s].reshape(size, width)
            both = jnp.dot(taps_mat[...], cells, preferred_element_type=jnp.float32)
            live = jnp.where(q * CHUNK + s < live_count, 1.0, 0.0)
            filtered = (both[:size] + both[size:]) * live
            send_x[q, :, :, s] = filtered.astype(jnp.bfloat16).reshape(lanes, 2, block, width)
        for d in (2, 1, 3):
            x_copy(q, f_peer(d), my_f).start()
        land_x[q, my_f] = send_x[q, my_f]
        return carry

    def out_copy(q):
        return pltpu.make_async_copy(
            result.at[q], out_ref.at[:, 0, pl.ds(q * CHUNK, CHUNK)], out_sem.at[q]
        )

    def fit_pair(p):
        for half in range(2):
            q = 2 * p + half
            for d in range(1, lanes):
                x_copy(q, my_f, f_peer(d)).wait_recv()
            for j in range(lanes):
                gate = flag_ref[:, j * width : (j + 1) * width].astype(jnp.bfloat16)
                weighted[half * rows : (half + 1) * rows, j * width : (j + 1) * width] = (
                    land_x[q, j] * gate
                ).reshape(rows, width)

        def one_block(i, carry):
            fit = lax.dot_general(
                weighted[...],
                panels[i],
                (((1,), (1,)), ((), ())),
                preferred_element_type=jnp.float32,
            )
            columns = pl.ds(pl.multiple_of(i * width, width), width)
            for half in range(2):
                q = 2 * p + half
                slotted = land_x[q, i].astype(jnp.float32).reshape(rows, width)
                cleaned = (slotted - fit[half * rows : (half + 1) * rows]).astype(jnp.bfloat16)
                result[q, :, :, :, columns] = cleaned.reshape(2, CHUNK, block, width)
            return carry

        lax.fori_loop(0, lanes, one_block, 0)
        for half in range(2):
            out_copy(2 * p + half).start()

    early = chunks // 2
    lax.fori_loop(0, early, filter_chunk, 0)
    panel_copy(0, panel_ref.at[0], x_peer, my_f).wait_recv()
    forward = panel_copy(2, panels.at[x_peer], x_peer, core_peer)
    forward.start()
    filter_chunk(early, 0)
    panel_copy(1, panel_ref.at[0], core_peer, my_f).wait_recv()
    panel_copy(2, panel_ref.at[0], far_peer, my_f).wait_recv()
    own_panel.wait()
    fit_pair(0)

    def late(p, carry):
        filter_chunk(early + p, 0)
        fit_pair(p)
        return carry

    lax.fori_loop(1, early, late, 0)

    def finish(q, carry):
        out_copy(q).wait()
        for d in range(1, groups):
            z_copy(q, z_peer(d), my_z).wait_send()
        for d in range(1, lanes):
            x_copy(q, f_peer(d), my_f).wait_send()
        return carry

    lax.fori_loop(0, chunks, finish, 0)
    to_x.wait_send()
    to_core.wait_send()
    forward.wait_send()


def kernel_shards(
    groups, lanes, visibilities, class_ids, class_counts, tap_windows, fringe_taps, flag_mask, filter_panels
):
    block, width = visibilities.shape[2:]
    channels = lanes * width
    chunks = SLOTS // CHUNK
    size = 2 * groups * block
    bf16 = jnp.bfloat16
    smem = pl.BlockSpec(memory_space=pltpu.SMEM)
    vmem = pl.BlockSpec(memory_space=pltpu.VMEM)
    hbm = pl.BlockSpec(memory_space=pl.ANY)
    dma = pltpu.SemaphoreType.DMA
    return pl.pallas_call(
        functools.partial(kernel, groups, lanes),
        out_shape=jax.ShapeDtypeStruct((2, 1, SLOTS, block, channels), bf16),
        in_specs=[smem, smem, smem, vmem, vmem, hbm],
        out_specs=hbm,
        scratch_shapes=[
            pltpu.VMEM((chunks, groups, 2, CHUNK, block, width), bf16),
            pltpu.VMEM((chunks, groups, 2, CHUNK, block, width), bf16),
            pltpu.VMEM((chunks, lanes, 2, CHUNK, block, width), bf16),
            pltpu.VMEM((chunks, lanes, 2, CHUNK, block, width), bf16),
            pltpu.VMEM((lanes, width, channels), bf16),
            pltpu.VMEM((2 * size, size), bf16),
            pltpu.VMEM((4 * CHUNK * block, channels), bf16),
            pltpu.VMEM((chunks, 2, CHUNK, block, channels), bf16),
            dma((chunks, groups)),
            dma((chunks, groups)),
            dma((chunks, lanes)),
            dma((chunks, lanes)),
            dma((3,)),
            dma((3,)),
            dma,
            dma((chunks,)),
        ],
        compiler_params=pltpu.CompilerParams(
            collective_id=0, has_side_effects=True, vmem_limit_bytes=44 * 2**20
        ),
        cost_estimate=pl.CostEstimate(
            flops=2 * 2 * SLOTS * block * channels * channels,
            bytes_accessed=4 * SLOTS * block * channels * 2,
            transcendentals=0,
        ),
    )(class_counts, tap_windows, fringe_taps, visibilities, flag_mask, filter_panels)


def shards(*arrays):
    visibilities, panels = arrays[0], arrays[6]
    groups, lanes = lax.axis_size("tm"), lax.axis_size("freq")
    block, width = visibilities.shape[2:]
    fits = (
        groups == 4
        and lanes == 4
        and panels.shape[0] == 1
        and arrays[5].shape[0] == block
        and block % 16 == 0
        and width % 128 == 0
    )
    if fits:
        return kernel_shards(groups, lanes, *arrays)
    return plain_shards(*arrays)


def solution(mesh):
    return jax.shard_map(
        shards,
        mesh=mesh,
        in_specs=(
            P(None, "grp", "tm", "freq"),
            P("grp"),
            P("grp"),
            P("grp"),
            P(None, "grp", None),
            P("freq", None),
            P(("grp", "tm"), "freq", None),
        ),
        out_specs=P(None, ("grp", "tm"), None, "freq", None),
        check_vma=False,
    )
```

```python
import functools

import jax
import jax.numpy as jnp
from jax import lax
from jax.experimental import pallas as pl
from jax.experimental.pallas import tpu as pltpu
from jax.sharding import PartitionSpec as P

SLOTS = 32
REACH = 4
CHUNK = 2
GROUP = 4
MESH = pl.DeviceIdType.MESH


def extended(cells, sides, width):
    for axis, dim in sides:
        count = lax.axis_size(axis)
        ends = count - 1
        head = lax.slice_in_dim(cells, 0, width, axis=dim)
        tail = lax.slice_in_dim(cells, cells.shape[dim] - width, cells.shape[dim], axis=dim)
        cells = jnp.concatenate(
            [
                lax.ppermute(tail, axis, [(i, (i + 1) % count) for i in range(ends)]),
                cells,
                lax.ppermute(head, axis, [((i + 1) % count, i) for i in range(ends)]),
            ],
            axis=dim,
        )
    return cells


def masked_taps(fringe_taps, tap_windows):
    offsets = jnp.abs(jnp.arange(2 * REACH + 1, dtype=jnp.int32) - REACH)
    keep = (offsets[None, :] <= tap_windows[:, None]).astype(jnp.float32)
    return fringe_taps * keep[None, :, :]


def convolve(padded, row_taps, length):
    real_part = jnp.zeros(padded.shape[1:2] + (length,) + padded.shape[3:], jnp.float32)
    imag_part = jnp.zeros_like(real_part)
    for offset in range(2 * REACH + 1):
        shifted = lax.slice_in_dim(padded, 2 * REACH - offset, 2 * REACH - offset + length, axis=2)
        tap_real = row_taps[0, :, offset][:, None, None]
        tap_imag = row_taps[1, :, offset][:, None, None]
        real_part = real_part + tap_real * shifted[0] - tap_imag * shifted[1]
        imag_part = imag_part + tap_real * shifted[1] + tap_imag * shifted[0]
    return jnp.stack([real_part, imag_part]).astype(jnp.bfloat16)


def to_slots(per_baseline, class_counts):
    class_starts = jnp.cumsum(class_counts) - class_counts
    slot_positions = jnp.arange(SLOTS, dtype=jnp.int32)
    input_visibility = jnp.clip(
        class_starts[:, None] + slot_positions[None, :], 0, per_baseline.shape[1] - 1
    )
    live_slot = slot_positions[None, :] < class_counts[:, None]
    gathered = jnp.take(per_baseline, input_visibility.reshape(-1), axis=1)
    gathered = gathered.reshape(per_baseline.shape[:1] + live_slot.shape + per_baseline.shape[2:])
    return jnp.where(live_slot[None, :, :, None, None], gathered, jnp.zeros((), per_baseline.dtype))


def plain_shards(
    visibilities, class_ids, class_counts, tap_windows, fringe_taps, flag_mask, filter_panels
):
    taps_kept = masked_taps(fringe_taps, tap_windows)
    padded = extended(visibilities, (("tm", 2),), REACH)
    class_iota = jnp.arange(taps_kept.shape[1], dtype=jnp.int32)
    one_hot = (class_ids[:, None] == class_iota[None, :]).astype(jnp.float32)
    row_taps = jnp.einsum("bc,rck->rbk", one_hot, taps_kept, precision=lax.Precision.HIGHEST)
    filtered = convolve(padded, row_taps, visibilities.shape[2])
    slotted = to_slots(filtered, class_counts)
    local_block = lax.all_to_all(
        lax.all_to_all(slotted, "tm", split_axis=1, concat_axis=3, tiled=True),
        "freq",
        split_axis=3,
        concat_axis=4,
        tiled=True,
    )
    flag_gate = flag_mask.astype(jnp.bfloat16)
    weighted = local_block * flag_gate
    dayenu_fit = jnp.einsum(
        "rcstj,cij->rcsti",
        weighted,
        lax.all_gather(filter_panels, "freq", axis=1, tiled=True),
        preferred_element_type=jnp.float32,
    )
    return (local_block.astype(jnp.float32) - dayenu_fit).astype(jnp.bfloat16)


def tap_matrix(taps_ref, windows_ref, own_class, steps, block):
    size = 2 * steps
    out_pos = lax.broadcasted_iota(jnp.int32, (size, size), 0)
    in_pos = lax.broadcasted_iota(jnp.int32, (size, size), 1)

    def parts(pos):
        return (pos // (2 * block)) * block + pos % block, (pos // block) % 2

    out_t, out_r = parts(out_pos)
    in_t, in_r = parts(in_pos)
    lag = out_t - in_t
    same = out_r == in_r
    sign = (out_r - in_r).astype(jnp.float32)
    matrix = jnp.zeros((size, size), jnp.float32)
    window = windows_ref[own_class]
    for offset in range(2 * REACH + 1):
        keep = jnp.where(abs(offset - REACH) <= window, 1.0, 0.0)
        real = taps_ref[0, own_class, offset] * keep
        imag = taps_ref[1, own_class, offset] * keep
        value = jnp.where(same, real, sign * imag)
        matrix = jnp.where(lag == offset - REACH, value, matrix)
    return matrix


def kernel(
    groups,
    lanes,
    counts_ref,
    windows_ref,
    taps_ref,
    vis_hbm,
    flag_ref,
    panel_ref,
    out_ref,
    vis_ref,
    send_z,
    land_z,
    send_x,
    land_x,
    panels,
    panels_t,
    taps_mat,
    weighted,
    result,
    z_send_sem,
    z_recv_sem,
    x_send_sem,
    x_recv_sem,
    p_send_sem,
    p_recv_sem,
    local_sem,
    vis_sem,
    out_sem,
):
    my_z = lax.axis_index("tm")
    my_f = lax.axis_index("freq")
    chunks = SLOTS // CHUNK
    block = vis_ref.shape[2]
    width = vis_ref.shape[3]
    baselines = vis_ref.shape[1]
    rows = 2 * CHUNK * block

    def z_peer(d):
        return lax.rem(my_z + d, groups)

    def f_peer(d):
        return lax.rem(my_f + d, lanes)

    core_peer = my_f + 1 - 2 * lax.rem(my_f, 2)
    x_peer = f_peer(2)
    far_peer = core_peer + 2 - 4 * (core_peer // 2)

    fetch = pltpu.make_async_copy(vis_hbm, vis_ref, vis_sem)
    fetch.start()

    barrier = pltpu.get_barrier_semaphore()
    for d in range(1, groups):
        pl.semaphore_signal(barrier, inc=1, device_id={"tm": z_peer(d)}, device_id_type=MESH)
    for d in range(1, lanes):
        pl.semaphore_signal(barrier, inc=1, device_id={"freq": f_peer(d)}, device_id_type=MESH)
    pl.semaphore_wait(barrier, groups + lanes - 2)

    def panel_copy(which, source, owner, target):
        return pltpu.make_async_remote_copy(
            src_ref=source,
            dst_ref=panels.at[owner],
            send_sem=p_send_sem.at[which],
            recv_sem=p_recv_sem.at[which],
            device_id={"freq": target},
            device_id_type=MESH,
        )

    to_x = panel_copy(0, panel_ref.at[0], my_f, x_peer)
    to_core = panel_copy(1, panel_ref.at[0], my_f, core_peer)
    own_panel = pltpu.make_async_copy(panel_ref.at[0], panels.at[my_f], local_sem)

    def z_copy(q, target, source):
        return pltpu.make_async_remote_copy(
            src_ref=send_z.at[q, target],
            dst_ref=land_z.at[q, source],
            send_sem=z_send_sem.at[q, target],
            recv_sem=z_recv_sem.at[q, source],
            device_id={"tm": target},
            device_id_type=MESH,
        )

    def x_copy(q, target, source):
        return pltpu.make_async_remote_copy(
            src_ref=send_x.at[q, target],
            dst_ref=land_x.at[q, source],
            send_sem=x_send_sem.at[q, target],
            recv_sem=x_recv_sem.at[q, source],
            device_id={"freq": target},
            device_id_type=MESH,
        )

    def start_of(number):
        total = 0
        for i in range(groups):
            total = total + jnp.where(i < number, counts_ref[i], 0)
        return total

    starts = [start_of(z_peer(d)) for d in range(groups)]

    def pick(d, q, store):
        for s in range(CHUNK):
            row = jnp.minimum(starts[d] + q * CHUNK + s, baselines - 1)
            for r in range(2):
                store(r, s, vis_ref[r, row])

    def send_chunk(q, carry):
        for d in (2, 1, 3):
            target = z_peer(d)

            def store(r, s, value):
                send_z[q, target, r, s] = value

            pick(d, q, store)
            z_copy(q, target, my_z).start()
        return carry

    fetch.wait()
    send_chunk(0, 0)
    to_x.start()
    to_core.start()
    own_panel.start()
    lax.fori_loop(1, chunks, send_chunk, 0)

    def keep_chunk(q, carry):
        def store(r, s, value):
            land_z[q, my_z, r, s] = value

        pick(0, q, store)
        return carry

    lax.fori_loop(0, chunks, keep_chunk, 0)

    full = tap_matrix(taps_ref, windows_ref, my_z, groups * block, block)
    size = 2 * groups * block
    high = full.astype(jnp.bfloat16)
    taps_mat[:size, :] = high
    taps_mat[size:, :] = (full - high.astype(jnp.float32)).astype(jnp.bfloat16)
    live_count = counts_ref[my_z]

    def filter_chunk(q, carry):
        for d in range(1, groups):
            z_copy(q, my_z, z_peer(d)).wait_recv()
        for s in range(CHUNK):
            cells = land_z[q, :, :, s].reshape(size, width)
            both = jnp.dot(taps_mat[...], cells, preferred_element_type=jnp.float32)
            live = jnp.where(q * CHUNK + s < live_count, 1.0, 0.0)
            filtered = (both[:size] + both[size:]) * live
            send_x[q, :, :, s] = filtered.astype(jnp.bfloat16).reshape(lanes, 2, block, width)
        for d in (2, 1, 3):
            x_copy(q, f_peer(d), my_f).start()
        land_x[q, my_f] = send_x[q, my_f]
        return carry

    def out_copy(q):
        return pltpu.make_async_copy(
            result.at[q], out_ref.at[:, 0, pl.ds(q * CHUNK, CHUNK)], out_sem.at[q]
        )

    def fit_chunks(first, count):
        for h in range(count):
            for d in range(1, lanes):
                x_copy(first + h, my_f, f_peer(d)).wait_recv()
            for j in range(lanes):
                gate = flag_ref[:, j * width : (j + 1) * width].astype(jnp.bfloat16)
                weighted[h * rows : (h + 1) * rows, j * width : (j + 1) * width] = (
                    land_x[first + h, j] * gate
                ).reshape(rows, width)

        def one_block(i, carry):
            fit = jnp.dot(
                weighted[: count * rows], panels_t[i], preferred_element_type=jnp.float32
            )
            columns = pl.ds(pl.multiple_of(i * width, width), width)
            for h in range(count):
                slotted = land_x[first + h, i].astype(jnp.float32).reshape(rows, width)
                cleaned = (slotted - fit[h * rows : (h + 1) * rows]).astype(jnp.bfloat16)
                result[first + h, :, :, :, columns] = cleaned.reshape(2, CHUNK, block, width)
            return carry

        lax.fori_loop(0, lanes, one_block, 0)
        for h in range(count):
            out_copy(first + h).start()

    def turn(i, carry):
        panels_t[i] = panels[i].T
        return carry

    early = chunks // 2
    lax.fori_loop(0, early, filter_chunk, 0)
    panel_copy(0, panel_ref.at[0], x_peer, my_f).wait_recv()
    forward = panel_copy(2, panels.at[x_peer], x_peer, core_peer)
    forward.start()
    lax.fori_loop(early, early + 1, filter_chunk, 0)
    panel_copy(1, panel_ref.at[0], core_peer, my_f).wait_recv()
    panel_copy(2, panel_ref.at[0], far_peer, my_f).wait_recv()
    own_panel.wait()
    lax.fori_loop(0, lanes, turn, 0)

    def late(g, carry):
        fit_chunks(g * GROUP, GROUP)
        lax.fori_loop(early + 1 + 2 * g, early + 3 + 2 * g, filter_chunk, 0)
        return carry

    groups_done = chunks // GROUP - 1
    lax.fori_loop(0, groups_done, late, 0)
    done = groups_done * GROUP
    lax.fori_loop(early + 1 + 2 * groups_done, chunks - 1, filter_chunk, 0)
    fit_chunks(done, 2)
    lax.fori_loop(chunks - 1, chunks, filter_chunk, 0)

    def last(q, carry):
        fit_chunks(q, 1)
        return carry

    lax.fori_loop(done + 2, chunks, last, 0)

    def finish(q, carry):
        out_copy(q).wait()
        for d in range(1, groups):
            z_copy(q, z_peer(d), my_z).wait_send()
        for d in range(1, lanes):
            x_copy(q, f_peer(d), my_f).wait_send()
        return carry

    lax.fori_loop(0, chunks, finish, 0)
    to_x.wait_send()
    to_core.wait_send()
    forward.wait_send()


def kernel_shards(
    groups, lanes, visibilities, class_ids, class_counts, tap_windows, fringe_taps, flag_mask, filter_panels
):
    block, width = visibilities.shape[2:]
    channels = lanes * width
    chunks = SLOTS // CHUNK
    size = 2 * groups * block
    bf16 = jnp.bfloat16
    smem = pl.BlockSpec(memory_space=pltpu.SMEM)
    vmem = pl.BlockSpec(memory_space=pltpu.VMEM)
    hbm = pl.BlockSpec(memory_space=pl.ANY)
    dma = pltpu.SemaphoreType.DMA
    return pl.pallas_call(
        functools.partial(kernel, groups, lanes),
        out_shape=jax.ShapeDtypeStruct((2, 1, SLOTS, block, channels), bf16),
        in_specs=[smem, smem, smem, hbm, vmem, hbm],
        out_specs=hbm,
        scratch_shapes=[
            pltpu.VMEM(visibilities.shape, bf16),
            pltpu.VMEM((chunks, groups, 2, CHUNK, block, width), bf16),
            pltpu.VMEM((chunks, groups, 2, CHUNK, block, width), bf16),
            pltpu.VMEM((chunks, lanes, 2, CHUNK, block, width), bf16),
            pltpu.VMEM((chunks, lanes, 2, CHUNK, block, width), bf16),
            pltpu.VMEM((lanes, width, channels), bf16),
            pltpu.VMEM((lanes, channels, width), bf16),
            pltpu.VMEM((2 * size, size), bf16),
            pltpu.VMEM((GROUP * 2 * CHUNK * block, channels), bf16),
            pltpu.VMEM((chunks, 2, CHUNK, block, channels), bf16),
            dma((chunks, groups)),
            dma((chunks, groups)),
            dma((chunks, lanes)),
            dma((chunks, lanes)),
            dma((3,)),
            dma((3,)),
            dma,
            dma,
            dma((chunks,)),
        ],
        compiler_params=pltpu.CompilerParams(
            collective_id=0, has_side_effects=True, vmem_limit_bytes=60 * 2**20
        ),
        cost_estimate=pl.CostEstimate(
            flops=2 * 2 * SLOTS * block * channels * channels,
            bytes_accessed=4 * SLOTS * block * channels * 2,
            transcendentals=0,
        ),
    )(class_counts, tap_windows, fringe_taps, visibilities, flag_mask, filter_panels)


def shards(*arrays):
    visibilities, panels = arrays[0], arrays[6]
    groups, lanes = lax.axis_size("tm"), lax.axis_size("freq")
    block, width = visibilities.shape[2:]
    fits = (
        groups == 4
        and lanes == 4
        and panels.shape[0] == 1
        and arrays[5].shape[0] == block
        and block % 16 == 0
        and width % 128 == 0
    )
    if fits:
        return kernel_shards(groups, lanes, *arrays)
    return plain_shards(*arrays)


def solution(mesh):
    return jax.shard_map(
        shards,
        mesh=mesh,
        in_specs=(
            P(None, "grp", "tm", "freq"),
            P("grp"),
            P("grp"),
            P("grp"),
            P(None, "grp", None),
            P("freq", None),
            P(("grp", "tm"), "freq", None),
        ),
        out_specs=P(None, ("grp", "tm"), None, "freq", None),
        check_vma=False,
    )
```

```python
import functools

import jax
import jax.numpy as jnp
from jax import lax
from jax.experimental import pallas as pl
from jax.experimental.pallas import tpu as pltpu
from jax.sharding import PartitionSpec as P

SLOTS = 32
REACH = 4
CHUNK = 4
GROUP = 2
MESH = pl.DeviceIdType.MESH


def extended(cells, sides, width):
    for axis, dim in sides:
        count = lax.axis_size(axis)
        ends = count - 1
        head = lax.slice_in_dim(cells, 0, width, axis=dim)
        tail = lax.slice_in_dim(cells, cells.shape[dim] - width, cells.shape[dim], axis=dim)
        cells = jnp.concatenate(
            [
                lax.ppermute(tail, axis, [(i, (i + 1) % count) for i in range(ends)]),
                cells,
                lax.ppermute(head, axis, [((i + 1) % count, i) for i in range(ends)]),
            ],
            axis=dim,
        )
    return cells


def masked_taps(fringe_taps, tap_windows):
    offsets = jnp.abs(jnp.arange(2 * REACH + 1, dtype=jnp.int32) - REACH)
    keep = (offsets[None, :] <= tap_windows[:, None]).astype(jnp.float32)
    return fringe_taps * keep[None, :, :]


def convolve(padded, row_taps, length):
    real_part = jnp.zeros(padded.shape[1:2] + (length,) + padded.shape[3:], jnp.float32)
    imag_part = jnp.zeros_like(real_part)
    for offset in range(2 * REACH + 1):
        shifted = lax.slice_in_dim(padded, 2 * REACH - offset, 2 * REACH - offset + length, axis=2)
        tap_real = row_taps[0, :, offset][:, None, None]
        tap_imag = row_taps[1, :, offset][:, None, None]
        real_part = real_part + tap_real * shifted[0] - tap_imag * shifted[1]
        imag_part = imag_part + tap_real * shifted[1] + tap_imag * shifted[0]
    return jnp.stack([real_part, imag_part]).astype(jnp.bfloat16)


def to_slots(per_baseline, class_counts):
    class_starts = jnp.cumsum(class_counts) - class_counts
    slot_positions = jnp.arange(SLOTS, dtype=jnp.int32)
    input_visibility = jnp.clip(
        class_starts[:, None] + slot_positions[None, :], 0, per_baseline.shape[1] - 1
    )
    live_slot = slot_positions[None, :] < class_counts[:, None]
    gathered = jnp.take(per_baseline, input_visibility.reshape(-1), axis=1)
    gathered = gathered.reshape(per_baseline.shape[:1] + live_slot.shape + per_baseline.shape[2:])
    return jnp.where(live_slot[None, :, :, None, None], gathered, jnp.zeros((), per_baseline.dtype))


def plain_shards(
    visibilities, class_ids, class_counts, tap_windows, fringe_taps, flag_mask, filter_panels
):
    taps_kept = masked_taps(fringe_taps, tap_windows)
    padded = extended(visibilities, (("tm", 2),), REACH)
    class_iota = jnp.arange(taps_kept.shape[1], dtype=jnp.int32)
    one_hot = (class_ids[:, None] == class_iota[None, :]).astype(jnp.float32)
    row_taps = jnp.einsum("bc,rck->rbk", one_hot, taps_kept, precision=lax.Precision.HIGHEST)
    filtered = convolve(padded, row_taps, visibilities.shape[2])
    slotted = to_slots(filtered, class_counts)
    local_block = lax.all_to_all(
        lax.all_to_all(slotted, "tm", split_axis=1, concat_axis=3, tiled=True),
        "freq",
        split_axis=3,
        concat_axis=4,
        tiled=True,
    )
    flag_gate = flag_mask.astype(jnp.bfloat16)
    weighted = local_block * flag_gate
    dayenu_fit = jnp.einsum(
        "rcstj,cij->rcsti",
        weighted,
        lax.all_gather(filter_panels, "freq", axis=1, tiled=True),
        preferred_element_type=jnp.float32,
    )
    return (local_block.astype(jnp.float32) - dayenu_fit).astype(jnp.bfloat16)


def tap_matrix(taps_ref, windows_ref, own_class, steps, block):
    size = 2 * steps
    out_pos = lax.broadcasted_iota(jnp.int32, (size, size), 0)
    in_pos = lax.broadcasted_iota(jnp.int32, (size, size), 1)

    def parts(pos):
        return (pos // (2 * block)) * block + pos % block, (pos // block) % 2

    out_t, out_r = parts(out_pos)
    in_t, in_r = parts(in_pos)
    lag = out_t - in_t
    same = out_r == in_r
    sign = (out_r - in_r).astype(jnp.float32)
    matrix = jnp.zeros((size, size), jnp.float32)
    window = windows_ref[own_class]
    for offset in range(2 * REACH + 1):
        keep = jnp.where(abs(offset - REACH) <= window, 1.0, 0.0)
        real = taps_ref[0, own_class, offset] * keep
        imag = taps_ref[1, own_class, offset] * keep
        value = jnp.where(same, real, sign * imag)
        matrix = jnp.where(lag == offset - REACH, value, matrix)
    return matrix


def kernel(
    groups,
    lanes,
    counts_hbm,
    windows_hbm,
    taps_hbm,
    vis_hbm,
    flag_hbm,
    panel_ref,
    out_ref,
    counts_ref,
    windows_ref,
    taps_ref,
    flag_ref,
    vis_ref,
    send_z,
    land_z,
    send_x,
    land_x,
    panels,
    panels_t,
    taps_mat,
    weighted,
    result,
    z_send_sem,
    z_recv_sem,
    x_send_sem,
    x_recv_sem,
    p_send_sem,
    p_recv_sem,
    local_sem,
    fetch_sem,
    out_sem,
):
    my_z = lax.axis_index("tm")
    my_f = lax.axis_index("freq")
    chunks = SLOTS // CHUNK
    block = vis_ref.shape[2]
    width = vis_ref.shape[3]
    baselines = vis_ref.shape[1]
    rows = 2 * CHUNK * block

    def z_peer(d):
        return lax.rem(my_z + d, groups)

    def f_peer(d):
        return lax.rem(my_f + d, lanes)

    core_peer = my_f + 1 - 2 * lax.rem(my_f, 2)
    x_peer = f_peer(2)
    far_peer = core_peer + 2 - 4 * (core_peer // 2)

    fetches = [
        pltpu.make_async_copy(source, target, fetch_sem.at[i])
        for i, (source, target) in enumerate(
            (
                (counts_hbm, counts_ref),
                (vis_hbm, vis_ref),
                (taps_hbm, taps_ref),
                (windows_hbm, windows_ref),
                (flag_hbm, flag_ref),
            )
        )
    ]
    for fetch in fetches:
        fetch.start()

    barrier = pltpu.get_barrier_semaphore()
    for d in range(1, groups):
        pl.semaphore_signal(barrier, inc=1, device_id={"tm": z_peer(d)}, device_id_type=MESH)
    for d in range(1, lanes):
        pl.semaphore_signal(barrier, inc=1, device_id={"freq": f_peer(d)}, device_id_type=MESH)
    pl.semaphore_wait(barrier, groups + lanes - 2)

    def panel_copy(which, source, owner, target):
        return pltpu.make_async_remote_copy(
            src_ref=source,
            dst_ref=panels.at[owner],
            send_sem=p_send_sem.at[which],
            recv_sem=p_recv_sem.at[which],
            device_id={"freq": target},
            device_id_type=MESH,
        )

    to_x = panel_copy(0, panel_ref.at[0], my_f, x_peer)
    to_core = panel_copy(1, panel_ref.at[0], my_f, core_peer)
    own_panel = pltpu.make_async_copy(panel_ref.at[0], panels.at[my_f], local_sem)

    def z_copy(q, target, source):
        return pltpu.make_async_remote_copy(
            src_ref=send_z.at[q, target],
            dst_ref=land_z.at[q, source],
            send_sem=z_send_sem.at[q, target],
            recv_sem=z_recv_sem.at[q, source],
            device_id={"tm": target},
            device_id_type=MESH,
        )

    def x_copy(q, target, source):
        return pltpu.make_async_remote_copy(
            src_ref=send_x.at[q, target],
            dst_ref=land_x.at[q, source],
            send_sem=x_send_sem.at[q, target],
            recv_sem=x_recv_sem.at[q, source],
            device_id={"freq": target},
            device_id_type=MESH,
        )

    def start_of(number):
        total = 0
        for i in range(groups):
            total = total + jnp.where(i < number, counts_ref[i], 0)
        return total

    def pick(number, q, store):
        first = start_of(number)
        for s in range(CHUNK):
            row = jnp.minimum(first + q * CHUNK + s, baselines - 1)
            for r in range(2):
                store(r, s, vis_ref[r, row])

    def send_chunk(q, target):
        def store(r, s, value):
            send_z[q, target, r, s] = value

        pick(target, q, store)
        z_copy(q, target, my_z).start()

    near = my_z + 1 - 2 * lax.rem(my_z, 2)
    across = (z_peer(2), lax.rem(near + 2, groups))
    inner = my_z % 3 != 0

    def send_near(q, carry):
        send_chunk(q, near)
        return carry

    def send_across(q, carry):
        for target in across:
            send_chunk(q, target)

        @pl.when(jnp.logical_and(inner, q >= chunks // 2))
        def _():
            send_chunk(2 * q - chunks, near)
            send_chunk(2 * q - chunks + 1, near)

        return carry

    fetches[0].wait()
    fetches[1].wait()
    send_chunk(0, jnp.where(inner, across[0], near))
    to_x.start()
    to_core.start()
    own_panel.start()

    @pl.when(inner)
    def _():
        send_chunk(0, across[1])

    @pl.when(jnp.logical_not(inner))
    def _():
        lax.fori_loop(1, chunks, send_near, 0)
        for target in across:
            send_chunk(0, target)

    lax.fori_loop(1, chunks, send_across, 0)
    for fetch in fetches[2:]:
        fetch.wait()

    def keep_chunk(q, carry):
        def store(r, s, value):
            land_z[q, my_z, r, s] = value

        pick(my_z, q, store)
        return carry

    lax.fori_loop(0, chunks, keep_chunk, 0)

    full = tap_matrix(taps_ref, windows_ref, my_z, groups * block, block)
    size = 2 * groups * block
    high = full.astype(jnp.bfloat16)
    taps_mat[:size, :] = high
    taps_mat[size:, :] = (full - high.astype(jnp.float32)).astype(jnp.bfloat16)
    live_count = counts_ref[my_z]

    def filter_chunk(q, carry):
        for d in range(1, groups):
            z_copy(q, my_z, z_peer(d)).wait_recv()
        for s in range(CHUNK):
            cells = land_z[q, :, :, s].reshape(size, width)
            both = jnp.dot(taps_mat[...], cells, preferred_element_type=jnp.float32)
            live = jnp.where(q * CHUNK + s < live_count, 1.0, 0.0)
            filtered = (both[:size] + both[size:]) * live
            send_x[q, :, :, s] = filtered.astype(jnp.bfloat16).reshape(lanes, 2, block, width)
        for d in (2, 1, 3):
            x_copy(q, f_peer(d), my_f).start()
        land_x[q, my_f] = send_x[q, my_f]
        return carry

    def out_copy(q):
        return pltpu.make_async_copy(
            result.at[q], out_ref.at[:, 0, pl.ds(q * CHUNK, CHUNK)], out_sem.at[q]
        )

    def fit_chunks(first, count):
        for h in range(count):
            for d in range(1, lanes):
                x_copy(first + h, my_f, f_peer(d)).wait_recv()
            for j in range(lanes):
                gate = flag_ref[:, j * width : (j + 1) * width].astype(jnp.bfloat16)
                weighted[h * rows : (h + 1) * rows, j * width : (j + 1) * width] = (
                    land_x[first + h, j] * gate
                ).reshape(rows, width)

        def one_block(i, carry):
            fit = jnp.dot(
                weighted[: count * rows], panels_t[i], preferred_element_type=jnp.float32
            )
            columns = pl.ds(pl.multiple_of(i * width, width), width)
            for h in range(count):
                slotted = land_x[first + h, i].astype(jnp.float32).reshape(rows, width)
                cleaned = (slotted - fit[h * rows : (h + 1) * rows]).astype(jnp.bfloat16)
                result[first + h, :, :, :, columns] = cleaned.reshape(2, CHUNK, block, width)
            return carry

        lax.fori_loop(0, lanes, one_block, 0)
        for h in range(count):
            out_copy(first + h).start()

    def turn(i, carry):
        panels_t[i] = panels[i].T
        return carry

    early = chunks // 2
    lax.fori_loop(0, early, filter_chunk, 0)
    panel_copy(0, panel_ref.at[0], x_peer, my_f).wait_recv()
    forward = panel_copy(2, panels.at[x_peer], x_peer, core_peer)
    forward.start()
    lax.fori_loop(early, early + 1, filter_chunk, 0)
    panel_copy(1, panel_ref.at[0], core_peer, my_f).wait_recv()
    panel_copy(2, panel_ref.at[0], far_peer, my_f).wait_recv()
    own_panel.wait()
    lax.fori_loop(0, lanes, turn, 0)

    def late(g, carry):
        fit_chunks(g * GROUP, GROUP)
        lax.fori_loop(early + 1 + g, early + 2 + g, filter_chunk, 0)
        return carry

    lax.fori_loop(0, early - 1, late, 0)

    def last(q, carry):
        fit_chunks(q, 1)
        return carry

    lax.fori_loop(chunks - GROUP, chunks, last, 0)

    def finish(q, carry):
        out_copy(q).wait()
        for d in range(1, groups):
            z_copy(q, z_peer(d), my_z).wait_send()
        for d in range(1, lanes):
            x_copy(q, f_peer(d), my_f).wait_send()
        return carry

    lax.fori_loop(0, chunks, finish, 0)
    to_x.wait_send()
    to_core.wait_send()
    forward.wait_send()


def kernel_shards(
    groups, lanes, visibilities, class_ids, class_counts, tap_windows, fringe_taps, flag_mask, filter_panels
):
    block, width = visibilities.shape[2:]
    channels = lanes * width
    chunks = SLOTS // CHUNK
    size = 2 * groups * block
    bf16 = jnp.bfloat16
    hbm = pl.BlockSpec(memory_space=pltpu.HBM)
    dma = pltpu.SemaphoreType.DMA
    return pl.pallas_call(
        functools.partial(kernel, groups, lanes),
        out_shape=jax.ShapeDtypeStruct((2, 1, SLOTS, block, channels), bf16),
        in_specs=[hbm] * 6,
        out_specs=pl.BlockSpec(memory_space=pl.ANY),
        scratch_shapes=[
            pltpu.SMEM(class_counts.shape, jnp.int32),
            pltpu.SMEM(tap_windows.shape, jnp.int32),
            pltpu.SMEM(fringe_taps.shape, jnp.float32),
            pltpu.VMEM(flag_mask.shape, jnp.int32),
            pltpu.VMEM(visibilities.shape, bf16),
            pltpu.VMEM((chunks, groups, 2, CHUNK, block, width), bf16),
            pltpu.VMEM((chunks, groups, 2, CHUNK, block, width), bf16),
            pltpu.VMEM((chunks, lanes, 2, CHUNK, block, width), bf16),
            pltpu.VMEM((chunks, lanes, 2, CHUNK, block, width), bf16),
            pltpu.VMEM((lanes, width, channels), bf16),
            pltpu.VMEM((lanes, channels, width), bf16),
            pltpu.VMEM((2 * size, size), bf16),
            pltpu.VMEM((GROUP * 2 * CHUNK * block, channels), bf16),
            pltpu.VMEM((chunks, 2, CHUNK, block, channels), bf16),
            dma((chunks, groups)),
            dma((chunks, groups)),
            dma((chunks, lanes)),
            dma((chunks, lanes)),
            dma((3,)),
            dma((3,)),
            dma,
            dma((5,)),
            dma((chunks,)),
        ],
        compiler_params=pltpu.CompilerParams(
            collective_id=0, has_side_effects=True, vmem_limit_bytes=60 * 2**20
        ),
        cost_estimate=pl.CostEstimate(
            flops=2 * 2 * SLOTS * block * channels * channels,
            bytes_accessed=4 * SLOTS * block * channels * 2,
            transcendentals=0,
        ),
    )(class_counts, tap_windows, fringe_taps, visibilities, flag_mask, filter_panels)


def shards(*arrays):
    visibilities, panels = arrays[0], arrays[6]
    groups, lanes = lax.axis_size("tm"), lax.axis_size("freq")
    block, width = visibilities.shape[2:]
    fits = (
        groups == 4
        and lanes == 4
        and panels.shape[0] == 1
        and arrays[5].shape[0] == block
        and block % 16 == 0
        and width % 128 == 0
    )
    if fits:
        return kernel_shards(groups, lanes, *arrays)
    return plain_shards(*arrays)


def solution(mesh):
    return jax.shard_map(
        shards,
        mesh=mesh,
        in_specs=(
            P(None, "grp", "tm", "freq"),
            P("grp"),
            P("grp"),
            P("grp"),
            P(None, "grp", None),
            P("freq", None),
            P(("grp", "tm"), "freq", None),
        ),
        out_specs=P(None, ("grp", "tm"), None, "freq", None),
        check_vma=False,
    )
```

```python
import functools

import jax
import jax.numpy as jnp
from jax import lax
from jax.experimental import pallas as pl
from jax.experimental.pallas import tpu as pltpu
from jax.sharding import PartitionSpec as P

SLOTS = 32
REACH = 4
CHUNK = 2
GROUP = 4
AHEAD = 6
MESH = pl.DeviceIdType.MESH


def extended(cells, sides, width):
    for axis, dim in sides:
        count = lax.axis_size(axis)
        ends = count - 1
        head = lax.slice_in_dim(cells, 0, width, axis=dim)
        tail = lax.slice_in_dim(cells, cells.shape[dim] - width, cells.shape[dim], axis=dim)
        cells = jnp.concatenate(
            [
                lax.ppermute(tail, axis, [(i, (i + 1) % count) for i in range(ends)]),
                cells,
                lax.ppermute(head, axis, [((i + 1) % count, i) for i in range(ends)]),
            ],
            axis=dim,
        )
    return cells


def masked_taps(fringe_taps, tap_windows):
    offsets = jnp.abs(jnp.arange(2 * REACH + 1, dtype=jnp.int32) - REACH)
    keep = (offsets[None, :] <= tap_windows[:, None]).astype(jnp.float32)
    return fringe_taps * keep[None, :, :]


def convolve(padded, row_taps, length):
    real_part = jnp.zeros(padded.shape[1:2] + (length,) + padded.shape[3:], jnp.float32)
    imag_part = jnp.zeros_like(real_part)
    for offset in range(2 * REACH + 1):
        shifted = lax.slice_in_dim(padded, 2 * REACH - offset, 2 * REACH - offset + length, axis=2)
        tap_real = row_taps[0, :, offset][:, None, None]
        tap_imag = row_taps[1, :, offset][:, None, None]
        real_part = real_part + tap_real * shifted[0] - tap_imag * shifted[1]
        imag_part = imag_part + tap_real * shifted[1] + tap_imag * shifted[0]
    return jnp.stack([real_part, imag_part]).astype(jnp.bfloat16)


def to_slots(per_baseline, class_counts):
    class_starts = jnp.cumsum(class_counts) - class_counts
    slot_positions = jnp.arange(SLOTS, dtype=jnp.int32)
    input_visibility = jnp.clip(
        class_starts[:, None] + slot_positions[None, :], 0, per_baseline.shape[1] - 1
    )
    live_slot = slot_positions[None, :] < class_counts[:, None]
    gathered = jnp.take(per_baseline, input_visibility.reshape(-1), axis=1)
    gathered = gathered.reshape(per_baseline.shape[:1] + live_slot.shape + per_baseline.shape[2:])
    return jnp.where(live_slot[None, :, :, None, None], gathered, jnp.zeros((), per_baseline.dtype))


def plain_shards(
    visibilities, class_ids, class_counts, tap_windows, fringe_taps, flag_mask, filter_panels
):
    taps_kept = masked_taps(fringe_taps, tap_windows)
    padded = extended(visibilities, (("tm", 2),), REACH)
    class_iota = jnp.arange(taps_kept.shape[1], dtype=jnp.int32)
    one_hot = (class_ids[:, None] == class_iota[None, :]).astype(jnp.float32)
    row_taps = jnp.einsum("bc,rck->rbk", one_hot, taps_kept, precision=lax.Precision.HIGHEST)
    filtered = convolve(padded, row_taps, visibilities.shape[2])
    slotted = to_slots(filtered, class_counts)
    local_block = lax.all_to_all(
        lax.all_to_all(slotted, "tm", split_axis=1, concat_axis=3, tiled=True),
        "freq",
        split_axis=3,
        concat_axis=4,
        tiled=True,
    )
    flag_gate = flag_mask.astype(jnp.bfloat16)
    weighted = local_block * flag_gate
    dayenu_fit = jnp.einsum(
        "rcstj,cij->rcsti",
        weighted,
        lax.all_gather(filter_panels, "freq", axis=1, tiled=True),
        preferred_element_type=jnp.float32,
    )
    return (local_block.astype(jnp.float32) - dayenu_fit).astype(jnp.bfloat16)


def tap_matrix(taps_ref, windows_ref, own_class, steps, block):
    size = 2 * steps
    out_pos = lax.broadcasted_iota(jnp.int32, (size, size), 0)
    in_pos = lax.broadcasted_iota(jnp.int32, (size, size), 1)

    def parts(pos):
        return (pos // (2 * block)) * block + pos % block, (pos // block) % 2

    out_t, out_r = parts(out_pos)
    in_t, in_r = parts(in_pos)
    lag = out_t - in_t
    same = out_r == in_r
    sign = (out_r - in_r).astype(jnp.float32)
    matrix = jnp.zeros((size, size), jnp.float32)
    window = windows_ref[own_class]
    for offset in range(2 * REACH + 1):
        keep = jnp.where(abs(offset - REACH) <= window, 1.0, 0.0)
        real = taps_ref[0, own_class, offset] * keep
        imag = taps_ref[1, own_class, offset] * keep
        value = jnp.where(same, real, sign * imag)
        matrix = jnp.where(lag == offset - REACH, value, matrix)
    return matrix


def kernel(
    groups,
    lanes,
    counts_hbm,
    windows_hbm,
    taps_hbm,
    vis_hbm,
    flag_hbm,
    panel_ref,
    out_ref,
    counts_ref,
    windows_ref,
    taps_ref,
    flag_ref,
    vis_ref,
    send_z,
    land_z,
    send_x,
    land_x,
    panels,
    panels_t,
    taps_mat,
    weighted,
    result,
    z_send_sem,
    z_recv_sem,
    x_send_sem,
    x_recv_sem,
    p_send_sem,
    p_recv_sem,
    local_sem,
    fetch_sem,
    out_sem,
):
    my_z = lax.axis_index("tm")
    my_f = lax.axis_index("freq")
    chunks = SLOTS // CHUNK
    block = vis_ref.shape[2]
    width = vis_ref.shape[3]
    baselines = vis_ref.shape[1]
    rows = 2 * CHUNK * block

    def z_peer(d):
        return lax.rem(my_z + d, groups)

    def f_peer(d):
        return lax.rem(my_f + d, lanes)

    core_peer = my_f + 1 - 2 * lax.rem(my_f, 2)
    x_peer = f_peer(2)
    far_peer = core_peer + 2 - 4 * (core_peer // 2)

    fetches = [
        pltpu.make_async_copy(source, target, fetch_sem.at[i])
        for i, (source, target) in enumerate(
            (
                (counts_hbm, counts_ref),
                (vis_hbm, vis_ref),
                (taps_hbm, taps_ref),
                (windows_hbm, windows_ref),
                (flag_hbm, flag_ref),
            )
        )
    ]
    for fetch in fetches:
        fetch.start()

    barrier = pltpu.get_barrier_semaphore()
    for d in range(1, groups):
        pl.semaphore_signal(barrier, inc=1, device_id={"tm": z_peer(d)}, device_id_type=MESH)
    for d in range(1, lanes):
        pl.semaphore_signal(barrier, inc=1, device_id={"freq": f_peer(d)}, device_id_type=MESH)
    pl.semaphore_wait(barrier, groups + lanes - 2)

    def panel_copy(which, source, owner, target):
        return pltpu.make_async_remote_copy(
            src_ref=source,
            dst_ref=panels.at[owner],
            send_sem=p_send_sem.at[which],
            recv_sem=p_recv_sem.at[which],
            device_id={"freq": target},
            device_id_type=MESH,
        )

    to_x = panel_copy(0, panel_ref.at[0], my_f, x_peer)
    to_core = panel_copy(1, panel_ref.at[0], my_f, core_peer)
    own_panel = pltpu.make_async_copy(panel_ref.at[0], panels.at[my_f], local_sem)

    def z_copy(q, target, source):
        return pltpu.make_async_remote_copy(
            src_ref=send_z.at[q, target],
            dst_ref=land_z.at[q, source],
            send_sem=z_send_sem.at[q, target],
            recv_sem=z_recv_sem.at[q, source],
            device_id={"tm": target},
            device_id_type=MESH,
        )

    def x_copy(q, target, source):
        return pltpu.make_async_remote_copy(
            src_ref=send_x.at[q, target],
            dst_ref=land_x.at[q, source],
            send_sem=x_send_sem.at[q, target],
            recv_sem=x_recv_sem.at[q, source],
            device_id={"freq": target},
            device_id_type=MESH,
        )

    def start_of(number):
        total = 0
        for i in range(groups):
            total = total + jnp.where(i < number, counts_ref[i], 0)
        return total

    def pick(number, q, store):
        first = start_of(number)
        for s in range(CHUNK):
            row = jnp.minimum(first + q * CHUNK + s, baselines - 1)
            for r in range(2):
                store(r, s, vis_ref[r, row])

    def send_chunk(q, target):
        def store(r, s, value):
            send_z[q, target, r, s] = value

        pick(target, q, store)
        z_copy(q, target, my_z).start()

    near = my_z + 1 - 2 * lax.rem(my_z, 2)
    across = (z_peer(2), lax.rem(near + 2, groups))
    inner = my_z % 3 != 0

    def send_all(q, carry):
        send_chunk(q, near)
        for target in across:
            send_chunk(q, target)
        return carry

    fetches[0].wait()
    fetches[1].wait()
    send_all(0, 0)
    to_x.start()
    to_core.start()
    own_panel.start()
    lax.fori_loop(1, AHEAD, send_all, 0)

    @pl.when(jnp.logical_not(inner))
    def _():
        lax.fori_loop(AHEAD, chunks, send_all, 0)

    for fetch in fetches[2:]:
        fetch.wait()

    def keep_chunk(q, carry):
        def store(r, s, value):
            land_z[q, my_z, r, s] = value

        pick(my_z, q, store)
        return carry

    lax.fori_loop(0, chunks, keep_chunk, 0)

    full = tap_matrix(taps_ref, windows_ref, my_z, groups * block, block)
    size = 2 * groups * block
    high = full.astype(jnp.bfloat16)
    taps_mat[:size, :] = high
    taps_mat[size:, :] = (full - high.astype(jnp.float32)).astype(jnp.bfloat16)
    live_count = counts_ref[my_z]

    def filter_chunk(q, carry):
        for d in range(1, groups):
            z_copy(q, my_z, z_peer(d)).wait_recv()
        for s in range(CHUNK):
            cells = land_z[q, :, :, s].reshape(size, width)
            both = jnp.dot(taps_mat[...], cells, preferred_element_type=jnp.float32)
            live = jnp.where(q * CHUNK + s < live_count, 1.0, 0.0)
            filtered = (both[:size] + both[size:]) * live
            send_x[q, :, :, s] = filtered.astype(jnp.bfloat16).reshape(lanes, 2, block, width)
        for d in (2, 1, 3):
            x_copy(q, f_peer(d), my_f).start()
        land_x[q, my_f] = send_x[q, my_f]

        @pl.when(jnp.logical_and(inner, q + AHEAD < chunks))
        def _():
            send_all(q + AHEAD, 0)

        return carry

    def out_copy(q):
        return pltpu.make_async_copy(
            result.at[q], out_ref.at[:, 0, pl.ds(q * CHUNK, CHUNK)], out_sem.at[q]
        )

    def fit_chunks(first, count):
        for h in range(count):
            for d in range(1, lanes):
                x_copy(first + h, my_f, f_peer(d)).wait_recv()
            for j in range(lanes):
                gate = flag_ref[:, j * width : (j + 1) * width].astype(jnp.bfloat16)
                weighted[h * rows : (h + 1) * rows, j * width : (j + 1) * width] = (
                    land_x[first + h, j] * gate
                ).reshape(rows, width)

        def one_block(i, carry):
            fit = jnp.dot(
                weighted[: count * rows], panels_t[i], preferred_element_type=jnp.float32
            )
            columns = pl.ds(pl.multiple_of(i * width, width), width)
            for h in range(count):
                slotted = land_x[first + h, i].astype(jnp.float32).reshape(rows, width)
                cleaned = (slotted - fit[h * rows : (h + 1) * rows]).astype(jnp.bfloat16)
                result[first + h, :, :, :, columns] = cleaned.reshape(2, CHUNK, block, width)
            return carry

        lax.fori_loop(0, lanes, one_block, 0)
        for h in range(count):
            out_copy(first + h).start()

    def turn(i):
        panels_t[i] = panels[i].T

    def filter_chunks(first, last):
        lax.fori_loop(first, last, filter_chunk, 0)

    late = chunks - chunks // GROUP - 2
    filter_chunks(0, 1)
    own_panel.wait()
    turn(my_f)
    filter_chunks(1, 3)
    panel_copy(1, panel_ref.at[0], core_peer, my_f).wait_recv()
    turn(core_peer)
    filter_chunks(3, late)
    panel_copy(0, panel_ref.at[0], x_peer, my_f).wait_recv()
    forward = panel_copy(2, panels.at[x_peer], x_peer, core_peer)
    forward.start()
    turn(x_peer)
    filter_chunks(late, late + 1)
    panel_copy(2, panel_ref.at[0], far_peer, my_f).wait_recv()
    turn(far_peer)
    filter_chunks(late + 1, late + 2)

    def fit_group(g, carry):
        fit_chunks(g * GROUP, GROUP)
        filter_chunk(late + 2 + g, 0)
        return carry

    full_groups = chunks // GROUP - 1
    lax.fori_loop(0, full_groups, fit_group, 0)
    fit_chunks(full_groups * GROUP, GROUP // 2)
    filter_chunks(late + 2 + full_groups, chunks)

    def fit_one(q, carry):
        fit_chunks(q, 1)
        return carry

    lax.fori_loop(full_groups * GROUP + GROUP // 2, chunks, fit_one, 0)

    def finish(q, carry):
        out_copy(q).wait()
        for d in range(1, groups):
            z_copy(q, z_peer(d), my_z).wait_send()
        for d in range(1, lanes):
            x_copy(q, f_peer(d), my_f).wait_send()
        return carry

    lax.fori_loop(0, chunks, finish, 0)
    to_x.wait_send()
    to_core.wait_send()
    forward.wait_send()


def kernel_shards(
    groups, lanes, visibilities, class_ids, class_counts, tap_windows, fringe_taps, flag_mask, filter_panels
):
    block, width = visibilities.shape[2:]
    channels = lanes * width
    chunks = SLOTS // CHUNK
    size = 2 * groups * block
    bf16 = jnp.bfloat16
    hbm = pl.BlockSpec(memory_space=pltpu.HBM)
    dma = pltpu.SemaphoreType.DMA
    return pl.pallas_call(
        functools.partial(kernel, groups, lanes),
        out_shape=jax.ShapeDtypeStruct((2, 1, SLOTS, block, channels), bf16),
        in_specs=[hbm] * 6,
        out_specs=pl.BlockSpec(memory_space=pl.ANY),
        scratch_shapes=[
            pltpu.SMEM(class_counts.shape, jnp.int32),
            pltpu.SMEM(tap_windows.shape, jnp.int32),
            pltpu.SMEM(fringe_taps.shape, jnp.float32),
            pltpu.VMEM(flag_mask.shape, jnp.int32),
            pltpu.VMEM(visibilities.shape, bf16),
            pltpu.VMEM((chunks, groups, 2, CHUNK, block, width), bf16),
            pltpu.VMEM((chunks, groups, 2, CHUNK, block, width), bf16),
            pltpu.VMEM((chunks, lanes, 2, CHUNK, block, width), bf16),
            pltpu.VMEM((chunks, lanes, 2, CHUNK, block, width), bf16),
            pltpu.VMEM((lanes, width, channels), bf16),
            pltpu.VMEM((lanes, channels, width), bf16),
            pltpu.VMEM((2 * size, size), bf16),
            pltpu.VMEM((GROUP * 2 * CHUNK * block, channels), bf16),
            pltpu.VMEM((chunks, 2, CHUNK, block, channels), bf16),
            dma((chunks, groups)),
            dma((chunks, groups)),
            dma((chunks, lanes)),
            dma((chunks, lanes)),
            dma((3,)),
            dma((3,)),
            dma,
            dma((5,)),
            dma((chunks,)),
        ],
        compiler_params=pltpu.CompilerParams(
            collective_id=0, has_side_effects=True, vmem_limit_bytes=60 * 2**20
        ),
        cost_estimate=pl.CostEstimate(
            flops=2 * 2 * SLOTS * block * channels * channels,
            bytes_accessed=4 * SLOTS * block * channels * 2,
            transcendentals=0,
        ),
    )(class_counts, tap_windows, fringe_taps, visibilities, flag_mask, filter_panels)


def shards(*arrays):
    visibilities, panels = arrays[0], arrays[6]
    groups, lanes = lax.axis_size("tm"), lax.axis_size("freq")
    block, width = visibilities.shape[2:]
    fits = (
        groups == 4
        and lanes == 4
        and panels.shape[0] == 1
        and arrays[5].shape[0] == block
        and block % 16 == 0
        and width % 128 == 0
    )
    if fits:
        return kernel_shards(groups, lanes, *arrays)
    return plain_shards(*arrays)


def solution(mesh):
    return jax.shard_map(
        shards,
        mesh=mesh,
        in_specs=(
            P(None, "grp", "tm", "freq"),
            P("grp"),
            P("grp"),
            P("grp"),
            P(None, "grp", None),
            P("freq", None),
            P(("grp", "tm"), "freq", None),
        ),
        out_specs=P(None, ("grp", "tm"), None, "freq", None),
        check_vma=False,
    )
```

```python
import functools

import jax
import jax.numpy as jnp
from jax import lax
from jax.experimental import pallas as pl
from jax.experimental.pallas import tpu as pltpu
from jax.sharding import PartitionSpec as P

SLOTS = 32
REACH = 4
CHUNK = 4
GROUP = 2
AHEAD = 3
MESH = pl.DeviceIdType.MESH


def extended(cells, sides, width):
    for axis, dim in sides:
        count = lax.axis_size(axis)
        ends = count - 1
        head = lax.slice_in_dim(cells, 0, width, axis=dim)
        tail = lax.slice_in_dim(cells, cells.shape[dim] - width, cells.shape[dim], axis=dim)
        cells = jnp.concatenate(
            [
                lax.ppermute(tail, axis, [(i, (i + 1) % count) for i in range(ends)]),
                cells,
                lax.ppermute(head, axis, [((i + 1) % count, i) for i in range(ends)]),
            ],
            axis=dim,
        )
    return cells


def masked_taps(fringe_taps, tap_windows):
    offsets = jnp.abs(jnp.arange(2 * REACH + 1, dtype=jnp.int32) - REACH)
    keep = (offsets[None, :] <= tap_windows[:, None]).astype(jnp.float32)
    return fringe_taps * keep[None, :, :]


def convolve(padded, row_taps, length):
    real_part = jnp.zeros(padded.shape[1:2] + (length,) + padded.shape[3:], jnp.float32)
    imag_part = jnp.zeros_like(real_part)
    for offset in range(2 * REACH + 1):
        shifted = lax.slice_in_dim(padded, 2 * REACH - offset, 2 * REACH - offset + length, axis=2)
        tap_real = row_taps[0, :, offset][:, None, None]
        tap_imag = row_taps[1, :, offset][:, None, None]
        real_part = real_part + tap_real * shifted[0] - tap_imag * shifted[1]
        imag_part = imag_part + tap_real * shifted[1] + tap_imag * shifted[0]
    return jnp.stack([real_part, imag_part]).astype(jnp.bfloat16)


def to_slots(per_baseline, class_counts):
    class_starts = jnp.cumsum(class_counts) - class_counts
    slot_positions = jnp.arange(SLOTS, dtype=jnp.int32)
    input_visibility = jnp.clip(
        class_starts[:, None] + slot_positions[None, :], 0, per_baseline.shape[1] - 1
    )
    live_slot = slot_positions[None, :] < class_counts[:, None]
    gathered = jnp.take(per_baseline, input_visibility.reshape(-1), axis=1)
    gathered = gathered.reshape(per_baseline.shape[:1] + live_slot.shape + per_baseline.shape[2:])
    return jnp.where(live_slot[None, :, :, None, None], gathered, jnp.zeros((), per_baseline.dtype))


def plain_shards(
    visibilities, class_ids, class_counts, tap_windows, fringe_taps, flag_mask, filter_panels
):
    taps_kept = masked_taps(fringe_taps, tap_windows)
    padded = extended(visibilities, (("tm", 2),), REACH)
    class_iota = jnp.arange(taps_kept.shape[1], dtype=jnp.int32)
    one_hot = (class_ids[:, None] == class_iota[None, :]).astype(jnp.float32)
    row_taps = jnp.einsum("bc,rck->rbk", one_hot, taps_kept, precision=lax.Precision.HIGHEST)
    filtered = convolve(padded, row_taps, visibilities.shape[2])
    slotted = to_slots(filtered, class_counts)
    local_block = lax.all_to_all(
        lax.all_to_all(slotted, "tm", split_axis=1, concat_axis=3, tiled=True),
        "freq",
        split_axis=3,
        concat_axis=4,
        tiled=True,
    )
    flag_gate = flag_mask.astype(jnp.bfloat16)
    weighted = local_block * flag_gate
    dayenu_fit = jnp.einsum(
        "rcstj,cij->rcsti",
        weighted,
        lax.all_gather(filter_panels, "freq", axis=1, tiled=True),
        preferred_element_type=jnp.float32,
    )
    return (local_block.astype(jnp.float32) - dayenu_fit).astype(jnp.bfloat16)


def tap_matrix(taps_ref, windows_ref, own_class, steps, block):
    size = 2 * steps
    out_pos = lax.broadcasted_iota(jnp.int32, (size, size), 0)
    in_pos = lax.broadcasted_iota(jnp.int32, (size, size), 1)

    def parts(pos):
        return (pos // (2 * block)) * block + pos % block, (pos // block) % 2

    out_t, out_r = parts(out_pos)
    in_t, in_r = parts(in_pos)
    lag = out_t - in_t
    same = out_r == in_r
    sign = (out_r - in_r).astype(jnp.float32)
    matrix = jnp.zeros((size, size), jnp.float32)
    window = windows_ref[own_class]
    for offset in range(2 * REACH + 1):
        keep = jnp.where(abs(offset - REACH) <= window, 1.0, 0.0)
        real = taps_ref[0, own_class, offset] * keep
        imag = taps_ref[1, own_class, offset] * keep
        value = jnp.where(same, real, sign * imag)
        matrix = jnp.where(lag == offset - REACH, value, matrix)
    return matrix


def kernel(
    groups,
    lanes,
    counts_hbm,
    windows_hbm,
    taps_hbm,
    vis_hbm,
    flag_hbm,
    panel_ref,
    out_ref,
    counts_ref,
    windows_ref,
    taps_ref,
    flag_ref,
    vis_ref,
    send_z,
    land_z,
    send_x,
    land_x,
    panels,
    panels_t,
    taps_mat,
    weighted,
    result,
    z_send_sem,
    z_recv_sem,
    x_send_sem,
    x_recv_sem,
    p_send_sem,
    p_recv_sem,
    local_sem,
    fetch_sem,
    out_sem,
):
    my_z = lax.axis_index("tm")
    my_f = lax.axis_index("freq")
    chunks = SLOTS // CHUNK
    block = vis_ref.shape[2]
    width = vis_ref.shape[3]
    baselines = vis_ref.shape[1]
    rows = 2 * CHUNK * block

    def z_peer(d):
        return lax.rem(my_z + d, groups)

    def f_peer(d):
        return lax.rem(my_f + d, lanes)

    core_peer = my_f + 1 - 2 * lax.rem(my_f, 2)
    x_peer = f_peer(2)
    far_peer = core_peer + 2 - 4 * (core_peer // 2)

    fetches = [
        pltpu.make_async_copy(source, target, fetch_sem.at[i])
        for i, (source, target) in enumerate(
            (
                (counts_hbm, counts_ref),
                (vis_hbm, vis_ref),
                (taps_hbm, taps_ref),
                (windows_hbm, windows_ref),
                (flag_hbm, flag_ref),
            )
        )
    ]
    for fetch in fetches:
        fetch.start()

    barrier = pltpu.get_barrier_semaphore()
    for d in range(1, groups):
        pl.semaphore_signal(barrier, inc=1, device_id={"tm": z_peer(d)}, device_id_type=MESH)
    for d in range(1, lanes):
        pl.semaphore_signal(barrier, inc=1, device_id={"freq": f_peer(d)}, device_id_type=MESH)
    pl.semaphore_wait(barrier, groups + lanes - 2)

    def panel_copy(which, source, owner, target):
        return pltpu.make_async_remote_copy(
            src_ref=source,
            dst_ref=panels.at[owner],
            send_sem=p_send_sem.at[which],
            recv_sem=p_recv_sem.at[which],
            device_id={"freq": target},
            device_id_type=MESH,
        )

    to_x = panel_copy(0, panel_ref.at[0], my_f, x_peer)
    to_core = panel_copy(1, panel_ref.at[0], my_f, core_peer)
    own_panel = pltpu.make_async_copy(panel_ref.at[0], panels.at[my_f], local_sem)

    def z_copy(q, target, source):
        return pltpu.make_async_remote_copy(
            src_ref=send_z.at[q, target],
            dst_ref=land_z.at[q, source],
            send_sem=z_send_sem.at[q, target],
            recv_sem=z_recv_sem.at[q, source],
            device_id={"tm": target},
            device_id_type=MESH,
        )

    def x_copy(q, target, source):
        return pltpu.make_async_remote_copy(
            src_ref=send_x.at[q, target],
            dst_ref=land_x.at[q, source],
            send_sem=x_send_sem.at[q, target],
            recv_sem=x_recv_sem.at[q, source],
            device_id={"freq": target},
            device_id_type=MESH,
        )

    def start_of(number):
        total = 0
        for i in range(groups):
            total = total + jnp.where(i < number, counts_ref[i], 0)
        return total

    def pick(number, q, store):
        first = start_of(number)
        for s in range(CHUNK):
            row = jnp.minimum(first + q * CHUNK + s, baselines - 1)
            for r in range(2):
                store(r, s, vis_ref[r, row])

    def send_chunk(q, target):
        def store(r, s, value):
            send_z[q, target, r, s] = value

        pick(target, q, store)
        z_copy(q, target, my_z).start()

    near = my_z + 1 - 2 * lax.rem(my_z, 2)
    across = (z_peer(2), lax.rem(near + 2, groups))

    def send_all(q, carry):
        send_chunk(q, near)
        for target in across:
            send_chunk(q, target)
        return carry

    fetches[0].wait()
    fetches[1].wait()
    send_all(0, 0)
    to_x.start()
    to_core.start()
    own_panel.start()
    lax.fori_loop(1, AHEAD, send_all, 0)

    for fetch in fetches[2:]:
        fetch.wait()

    def keep_chunk(q, carry):
        def store(r, s, value):
            land_z[q, my_z, r, s] = value

        pick(my_z, q, store)
        return carry

    lax.fori_loop(0, chunks, keep_chunk, 0)

    full = tap_matrix(taps_ref, windows_ref, my_z, groups * block, block)
    size = 2 * groups * block
    high = full.astype(jnp.bfloat16)
    taps_mat[:size, :] = high
    taps_mat[size:, :] = (full - high.astype(jnp.float32)).astype(jnp.bfloat16)
    live_count = counts_ref[my_z]

    def filter_chunk(q, carry):
        for d in range(1, groups):
            z_copy(q, my_z, z_peer(d)).wait_recv()
        for s in range(CHUNK):
            cells = land_z[q, :, :, s].reshape(size, width)
            both = jnp.dot(taps_mat[...], cells, preferred_element_type=jnp.float32)
            live = jnp.where(q * CHUNK + s < live_count, 1.0, 0.0)
            filtered = (both[:size] + both[size:]) * live
            send_x[q, :, :, s] = filtered.astype(jnp.bfloat16).reshape(lanes, 2, block, width)
        for d in (2, 1, 3):
            x_copy(q, f_peer(d), my_f).start()
        land_x[q, my_f] = send_x[q, my_f]

        @pl.when(q + AHEAD < chunks)
        def _():
            send_all(q + AHEAD, 0)

        return carry

    def out_copy(q):
        return pltpu.make_async_copy(
            result.at[q], out_ref.at[:, 0, pl.ds(q * CHUNK, CHUNK)], out_sem.at[q]
        )

    def fit_chunks(first, count):
        for h in range(count):
            for d in range(1, lanes):
                x_copy(first + h, my_f, f_peer(d)).wait_recv()
            for j in range(lanes):
                gate = flag_ref[:, j * width : (j + 1) * width].astype(jnp.bfloat16)
                weighted[h * rows : (h + 1) * rows, j * width : (j + 1) * width] = (
                    land_x[first + h, j] * gate
                ).reshape(rows, width)

        def one_block(i, carry):
            fit = jnp.dot(
                weighted[: count * rows], panels_t[i], preferred_element_type=jnp.float32
            )
            columns = pl.ds(pl.multiple_of(i * width, width), width)
            for h in range(count):
                slotted = land_x[first + h, i].astype(jnp.float32).reshape(rows, width)
                cleaned = (slotted - fit[h * rows : (h + 1) * rows]).astype(jnp.bfloat16)
                result[first + h, :, :, :, columns] = cleaned.reshape(2, CHUNK, block, width)
            return carry

        lax.fori_loop(0, lanes, one_block, 0)
        for h in range(count):
            out_copy(first + h).start()

    def turn(i):
        panels_t[i] = panels[i].T

    def filter_chunks(first, last):
        lax.fori_loop(first, last, filter_chunk, 0)

    half = chunks // 2
    filter_chunks(0, 1)
    own_panel.wait()
    turn(my_f)
    filter_chunks(1, 2)
    panel_copy(1, panel_ref.at[0], core_peer, my_f).wait_recv()
    turn(core_peer)
    filter_chunks(2, half + 1)
    panel_copy(0, panel_ref.at[0], x_peer, my_f).wait_recv()
    forward = panel_copy(2, panels.at[x_peer], x_peer, core_peer)
    forward.start()
    turn(x_peer)
    filter_chunks(half + 1, half + 2)
    panel_copy(2, panel_ref.at[0], far_peer, my_f).wait_recv()
    turn(far_peer)

    def fit_group(g, carry):
        fit_chunks(g * GROUP, GROUP)
        return carry

    def fit_one(q, carry):
        fit_chunks(q, 1)
        return carry

    lax.fori_loop(0, 1, fit_group, 0)
    filter_chunks(half + 2, chunks - 1)
    lax.fori_loop(1, chunks // GROUP - 1, fit_group, 0)
    filter_chunks(chunks - 1, chunks)
    lax.fori_loop(chunks - GROUP, chunks, fit_one, 0)

    def finish(q, carry):
        out_copy(q).wait()
        for d in range(1, groups):
            z_copy(q, z_peer(d), my_z).wait_send()
        for d in range(1, lanes):
            x_copy(q, f_peer(d), my_f).wait_send()
        return carry

    lax.fori_loop(0, chunks, finish, 0)
    to_x.wait_send()
    to_core.wait_send()
    forward.wait_send()


def kernel_shards(
    groups, lanes, visibilities, class_ids, class_counts, tap_windows, fringe_taps, flag_mask, filter_panels
):
    block, width = visibilities.shape[2:]
    channels = lanes * width
    chunks = SLOTS // CHUNK
    size = 2 * groups * block
    bf16 = jnp.bfloat16
    hbm = pl.BlockSpec(memory_space=pltpu.HBM)
    dma = pltpu.SemaphoreType.DMA
    return pl.pallas_call(
        functools.partial(kernel, groups, lanes),
        out_shape=jax.ShapeDtypeStruct((2, 1, SLOTS, block, channels), bf16),
        in_specs=[hbm] * 6,
        out_specs=pl.BlockSpec(memory_space=pl.ANY),
        scratch_shapes=[
            pltpu.SMEM(class_counts.shape, jnp.int32),
            pltpu.SMEM(tap_windows.shape, jnp.int32),
            pltpu.SMEM(fringe_taps.shape, jnp.float32),
            pltpu.VMEM(flag_mask.shape, jnp.int32),
            pltpu.VMEM(visibilities.shape, bf16),
            pltpu.VMEM((chunks, groups, 2, CHUNK, block, width), bf16),
            pltpu.VMEM((chunks, groups, 2, CHUNK, block, width), bf16),
            pltpu.VMEM((chunks, lanes, 2, CHUNK, block, width), bf16),
            pltpu.VMEM((chunks, lanes, 2, CHUNK, block, width), bf16),
            pltpu.VMEM((lanes, width, channels), bf16),
            pltpu.VMEM((lanes, channels, width), bf16),
            pltpu.VMEM((2 * size, size), bf16),
            pltpu.VMEM((GROUP * 2 * CHUNK * block, channels), bf16),
            pltpu.VMEM((chunks, 2, CHUNK, block, channels), bf16),
            dma((chunks, groups)),
            dma((chunks, groups)),
            dma((chunks, lanes)),
            dma((chunks, lanes)),
            dma((3,)),
            dma((3,)),
            dma,
            dma((5,)),
            dma((chunks,)),
        ],
        compiler_params=pltpu.CompilerParams(
            collective_id=0, has_side_effects=True, vmem_limit_bytes=60 * 2**20
        ),
        cost_estimate=pl.CostEstimate(
            flops=2 * 2 * SLOTS * block * channels * channels,
            bytes_accessed=4 * SLOTS * block * channels * 2,
            transcendentals=0,
        ),
    )(class_counts, tap_windows, fringe_taps, visibilities, flag_mask, filter_panels)


def shards(*arrays):
    visibilities, panels = arrays[0], arrays[6]
    groups, lanes = lax.axis_size("tm"), lax.axis_size("freq")
    block, width = visibilities.shape[2:]
    fits = (
        groups == 4
        and lanes == 4
        and panels.shape[0] == 1
        and arrays[5].shape[0] == block
        and block % 16 == 0
        and width % 128 == 0
    )
    if fits:
        return kernel_shards(groups, lanes, *arrays)
    return plain_shards(*arrays)


def solution(mesh):
    return jax.shard_map(
        shards,
        mesh=mesh,
        in_specs=(
            P(None, "grp", "tm", "freq"),
            P("grp"),
            P("grp"),
            P("grp"),
            P(None, "grp", None),
            P("freq", None),
            P(("grp", "tm"), "freq", None),
        ),
        out_specs=P(None, ("grp", "tm"), None, "freq", None),
        check_vma=False,
    )
```

```python
import functools

import jax
import jax.numpy as jnp
from jax import lax
from jax.experimental import pallas as pl
from jax.experimental.pallas import tpu as pltpu
from jax.sharding import PartitionSpec as P

SLOTS = 32
REACH = 4
CHUNK = 2
GROUP = 4
AHEAD = 6
MESH = pl.DeviceIdType.MESH


def extended(cells, sides, width):
    for axis, dim in sides:
        count = lax.axis_size(axis)
        ends = count - 1
        head = lax.slice_in_dim(cells, 0, width, axis=dim)
        tail = lax.slice_in_dim(cells, cells.shape[dim] - width, cells.shape[dim], axis=dim)
        cells = jnp.concatenate(
            [
                lax.ppermute(tail, axis, [(i, (i + 1) % count) for i in range(ends)]),
                cells,
                lax.ppermute(head, axis, [((i + 1) % count, i) for i in range(ends)]),
            ],
            axis=dim,
        )
    return cells


def masked_taps(fringe_taps, tap_windows):
    offsets = jnp.abs(jnp.arange(2 * REACH + 1, dtype=jnp.int32) - REACH)
    keep = (offsets[None, :] <= tap_windows[:, None]).astype(jnp.float32)
    return fringe_taps * keep[None, :, :]


def convolve(padded, row_taps, length):
    real_part = jnp.zeros(padded.shape[1:2] + (length,) + padded.shape[3:], jnp.float32)
    imag_part = jnp.zeros_like(real_part)
    for offset in range(2 * REACH + 1):
        shifted = lax.slice_in_dim(padded, 2 * REACH - offset, 2 * REACH - offset + length, axis=2)
        tap_real = row_taps[0, :, offset][:, None, None]
        tap_imag = row_taps[1, :, offset][:, None, None]
        real_part = real_part + tap_real * shifted[0] - tap_imag * shifted[1]
        imag_part = imag_part + tap_real * shifted[1] + tap_imag * shifted[0]
    return jnp.stack([real_part, imag_part]).astype(jnp.bfloat16)


def to_slots(per_baseline, class_counts):
    class_starts = jnp.cumsum(class_counts) - class_counts
    slot_positions = jnp.arange(SLOTS, dtype=jnp.int32)
    input_visibility = jnp.clip(
        class_starts[:, None] + slot_positions[None, :], 0, per_baseline.shape[1] - 1
    )
    live_slot = slot_positions[None, :] < class_counts[:, None]
    gathered = jnp.take(per_baseline, input_visibility.reshape(-1), axis=1)
    gathered = gathered.reshape(per_baseline.shape[:1] + live_slot.shape + per_baseline.shape[2:])
    return jnp.where(live_slot[None, :, :, None, None], gathered, jnp.zeros((), per_baseline.dtype))


def plain_shards(
    visibilities, class_ids, class_counts, tap_windows, fringe_taps, flag_mask, filter_panels
):
    taps_kept = masked_taps(fringe_taps, tap_windows)
    padded = extended(visibilities, (("tm", 2),), REACH)
    class_iota = jnp.arange(taps_kept.shape[1], dtype=jnp.int32)
    one_hot = (class_ids[:, None] == class_iota[None, :]).astype(jnp.float32)
    row_taps = jnp.einsum("bc,rck->rbk", one_hot, taps_kept, precision=lax.Precision.HIGHEST)
    filtered = convolve(padded, row_taps, visibilities.shape[2])
    slotted = to_slots(filtered, class_counts)
    local_block = lax.all_to_all(
        lax.all_to_all(slotted, "tm", split_axis=1, concat_axis=3, tiled=True),
        "freq",
        split_axis=3,
        concat_axis=4,
        tiled=True,
    )
    flag_gate = flag_mask.astype(jnp.bfloat16)
    weighted = local_block * flag_gate
    dayenu_fit = jnp.einsum(
        "rcstj,cij->rcsti",
        weighted,
        lax.all_gather(filter_panels, "freq", axis=1, tiled=True),
        preferred_element_type=jnp.float32,
    )
    return (local_block.astype(jnp.float32) - dayenu_fit).astype(jnp.bfloat16)


def tap_matrix(taps_ref, windows_ref, own_class, steps, block):
    size = 2 * steps
    out_pos = lax.broadcasted_iota(jnp.int32, (size, size), 0)
    in_pos = lax.broadcasted_iota(jnp.int32, (size, size), 1)

    def parts(pos):
        return (pos // (2 * block)) * block + pos % block, (pos // block) % 2

    out_t, out_r = parts(out_pos)
    in_t, in_r = parts(in_pos)
    lag = out_t - in_t
    same = out_r == in_r
    sign = (out_r - in_r).astype(jnp.float32)
    matrix = jnp.zeros((size, size), jnp.float32)
    window = windows_ref[own_class]
    for offset in range(2 * REACH + 1):
        keep = jnp.where(abs(offset - REACH) <= window, 1.0, 0.0)
        real = taps_ref[0, own_class, offset] * keep
        imag = taps_ref[1, own_class, offset] * keep
        value = jnp.where(same, real, sign * imag)
        matrix = jnp.where(lag == offset - REACH, value, matrix)
    return matrix


def kernel(
    groups,
    lanes,
    counts_hbm,
    windows_hbm,
    taps_hbm,
    vis_hbm,
    flag_hbm,
    panel_ref,
    out_ref,
    counts_ref,
    windows_ref,
    taps_ref,
    flag_ref,
    vis_ref,
    send_z,
    land_z,
    send_x,
    land_x,
    panels,
    panels_t,
    taps_mat,
    weighted,
    result,
    z_send_sem,
    z_recv_sem,
    x_send_sem,
    x_recv_sem,
    p_send_sem,
    p_recv_sem,
    local_sem,
    fetch_sem,
    out_sem,
):
    my_z = lax.axis_index("tm")
    my_f = lax.axis_index("freq")
    chunks = SLOTS // CHUNK
    block = vis_ref.shape[2]
    width = vis_ref.shape[3]
    baselines = vis_ref.shape[1]
    rows = 2 * CHUNK * block

    def z_peer(d):
        return lax.rem(my_z + d, groups)

    def f_peer(d):
        return lax.rem(my_f + d, lanes)

    core_peer = my_f + 1 - 2 * lax.rem(my_f, 2)
    x_peer = f_peer(2)
    far_peer = core_peer + 2 - 4 * (core_peer // 2)

    fetches = [
        pltpu.make_async_copy(source, target, fetch_sem.at[i])
        for i, (source, target) in enumerate(
            (
                (counts_hbm, counts_ref),
                (vis_hbm, vis_ref),
                (taps_hbm, taps_ref),
                (windows_hbm, windows_ref),
                (flag_hbm, flag_ref),
            )
        )
    ]
    for fetch in fetches:
        fetch.start()

    barrier = pltpu.get_barrier_semaphore()
    for d in range(1, groups):
        pl.semaphore_signal(barrier, inc=1, device_id={"tm": z_peer(d)}, device_id_type=MESH)
    for d in range(1, lanes):
        pl.semaphore_signal(barrier, inc=1, device_id={"freq": f_peer(d)}, device_id_type=MESH)
    pl.semaphore_wait(barrier, groups + lanes - 2)

    def panel_copy(which, source, owner, target):
        return pltpu.make_async_remote_copy(
            src_ref=source,
            dst_ref=panels.at[owner],
            send_sem=p_send_sem.at[which],
            recv_sem=p_recv_sem.at[which],
            device_id={"freq": target},
            device_id_type=MESH,
        )

    to_x = panel_copy(0, panel_ref.at[0], my_f, x_peer)
    to_core = panel_copy(1, panel_ref.at[0], my_f, core_peer)
    own_panel = pltpu.make_async_copy(panel_ref.at[0], panels.at[my_f], local_sem)

    def z_copy(q, target, source):
        return pltpu.make_async_remote_copy(
            src_ref=send_z.at[q, target],
            dst_ref=land_z.at[q, source],
            send_sem=z_send_sem.at[q, target],
            recv_sem=z_recv_sem.at[q, source],
            device_id={"tm": target},
            device_id_type=MESH,
        )

    def x_copy(q, target, source):
        return pltpu.make_async_remote_copy(
            src_ref=send_x.at[q, target],
            dst_ref=land_x.at[q, source],
            send_sem=x_send_sem.at[q, target],
            recv_sem=x_recv_sem.at[q, source],
            device_id={"freq": target},
            device_id_type=MESH,
        )

    def start_of(number):
        total = 0
        for i in range(groups):
            total = total + jnp.where(i < number, counts_ref[i], 0)
        return total

    def pick(number, q, store):
        first = start_of(number)
        for s in range(CHUNK):
            row = jnp.minimum(first + q * CHUNK + s, baselines - 1)
            for r in range(2):
                store(r, s, vis_ref[r, row])

    def send_chunk(q, target):
        def store(r, s, value):
            send_z[q, target, r, s] = value

        pick(target, q, store)
        z_copy(q, target, my_z).start()

    near = my_z + 1 - 2 * lax.rem(my_z, 2)
    across = (z_peer(2), lax.rem(near + 2, groups))

    def send_all(q, carry):
        send_chunk(q, near)
        for target in across:
            send_chunk(q, target)
        return carry

    fetches[0].wait()
    fetches[1].wait()
    send_all(0, 0)
    to_x.start()
    to_core.start()
    own_panel.start()
    lax.fori_loop(1, AHEAD, send_all, 0)

    for fetch in fetches[2:]:
        fetch.wait()

    def keep_chunk(q, carry):
        def store(r, s, value):
            land_z[q, my_z, r, s] = value

        pick(my_z, q, store)
        return carry

    lax.fori_loop(0, chunks, keep_chunk, 0)

    full = tap_matrix(taps_ref, windows_ref, my_z, groups * block, block)
    size = 2 * groups * block
    high = full.astype(jnp.bfloat16)
    taps_mat[:size, :] = high
    taps_mat[size:, :] = (full - high.astype(jnp.float32)).astype(jnp.bfloat16)
    live_count = counts_ref[my_z]

    def filter_chunk(q, carry):
        for d in range(1, groups):
            z_copy(q, my_z, z_peer(d)).wait_recv()
        for s in range(CHUNK):
            cells = land_z[q, :, :, s].reshape(size, width)
            both = jnp.dot(taps_mat[...], cells, preferred_element_type=jnp.float32)
            live = jnp.where(q * CHUNK + s < live_count, 1.0, 0.0)
            filtered = (both[:size] + both[size:]) * live
            send_x[q, :, :, s] = filtered.astype(jnp.bfloat16).reshape(lanes, 2, block, width)
        for d in (2, 1, 3):
            x_copy(q, f_peer(d), my_f).start()
        land_x[q, my_f] = send_x[q, my_f]

        @pl.when(q + AHEAD < chunks)
        def _():
            send_all(q + AHEAD, 0)

        return carry

    def out_copy(q):
        return pltpu.make_async_copy(
            result.at[q], out_ref.at[:, 0, pl.ds(q * CHUNK, CHUNK)], out_sem.at[q]
        )

    def fit_chunks(first, count):
        for h in range(count):
            for d in range(1, lanes):
                x_copy(first + h, my_f, f_peer(d)).wait_recv()
            for j in range(lanes):
                gate = flag_ref[:, j * width : (j + 1) * width].astype(jnp.bfloat16)
                weighted[h * rows : (h + 1) * rows, j * width : (j + 1) * width] = (
                    land_x[first + h, j] * gate
                ).reshape(rows, width)

        def one_block(i, carry):
            fit = jnp.dot(
                weighted[: count * rows], panels_t[i], preferred_element_type=jnp.float32
            )
            columns = pl.ds(pl.multiple_of(i * width, width), width)
            for h in range(count):
                slotted = land_x[first + h, i].astype(jnp.float32).reshape(rows, width)
                cleaned = (slotted - fit[h * rows : (h + 1) * rows]).astype(jnp.bfloat16)
                result[first + h, :, :, :, columns] = cleaned.reshape(2, CHUNK, block, width)
            return carry

        lax.fori_loop(0, lanes, one_block, 0)
        for h in range(count):
            out_copy(first + h).start()

    def turn(i):
        panels_t[i] = panels[i].T

    def filter_chunks(first, last):
        lax.fori_loop(first, last, filter_chunk, 0)

    full_groups = chunks // GROUP - 1
    late = chunks - full_groups - 3
    filter_chunks(0, 1)
    own_panel.wait()
    turn(my_f)
    filter_chunks(1, 3)
    panel_copy(1, panel_ref.at[0], core_peer, my_f).wait_recv()
    turn(core_peer)
    filter_chunks(3, late)
    panel_copy(0, panel_ref.at[0], x_peer, my_f).wait_recv()
    forward = panel_copy(2, panels.at[x_peer], x_peer, core_peer)
    forward.start()
    turn(x_peer)
    filter_chunks(late, late + 1)
    panel_copy(2, panel_ref.at[0], far_peer, my_f).wait_recv()
    turn(far_peer)
    filter_chunks(late + 1, late + 2)

    def fit_group(g, carry):
        fit_chunks(g * GROUP, GROUP)
        filter_chunk(late + 2 + g, 0)
        return carry

    def fit_one(q, carry):
        fit_chunks(q, 1)
        return carry

    lax.fori_loop(0, full_groups, fit_group, 0)
    fit_chunks(full_groups * GROUP, 2)
    filter_chunks(chunks - 1, chunks)
    lax.fori_loop(full_groups * GROUP + 2, chunks, fit_one, 0)

    def finish(q, carry):
        out_copy(q).wait()
        for d in range(1, groups):
            z_copy(q, z_peer(d), my_z).wait_send()
        for d in range(1, lanes):
            x_copy(q, f_peer(d), my_f).wait_send()
        return carry

    lax.fori_loop(0, chunks, finish, 0)
    to_x.wait_send()
    to_core.wait_send()
    forward.wait_send()


def kernel_shards(
    groups, lanes, visibilities, class_ids, class_counts, tap_windows, fringe_taps, flag_mask, filter_panels
):
    block, width = visibilities.shape[2:]
    channels = lanes * width
    chunks = SLOTS // CHUNK
    size = 2 * groups * block
    bf16 = jnp.bfloat16
    hbm = pl.BlockSpec(memory_space=pltpu.HBM)
    dma = pltpu.SemaphoreType.DMA
    return pl.pallas_call(
        functools.partial(kernel, groups, lanes),
        out_shape=jax.ShapeDtypeStruct((2, 1, SLOTS, block, channels), bf16),
        in_specs=[hbm] * 6,
        out_specs=pl.BlockSpec(memory_space=pl.ANY),
        scratch_shapes=[
            pltpu.SMEM(class_counts.shape, jnp.int32),
            pltpu.SMEM(tap_windows.shape, jnp.int32),
            pltpu.SMEM(fringe_taps.shape, jnp.float32),
            pltpu.VMEM(flag_mask.shape, jnp.int32),
            pltpu.VMEM(visibilities.shape, bf16),
            pltpu.VMEM((chunks, groups, 2, CHUNK, block, width), bf16),
            pltpu.VMEM((chunks, groups, 2, CHUNK, block, width), bf16),
            pltpu.VMEM((chunks, lanes, 2, CHUNK, block, width), bf16),
            pltpu.VMEM((chunks, lanes, 2, CHUNK, block, width), bf16),
            pltpu.VMEM((lanes, width, channels), bf16),
            pltpu.VMEM((lanes, channels, width), bf16),
            pltpu.VMEM((2 * size, size), bf16),
            pltpu.VMEM((GROUP * 2 * CHUNK * block, channels), bf16),
            pltpu.VMEM((chunks, 2, CHUNK, block, channels), bf16),
            dma((chunks, groups)),
            dma((chunks, groups)),
            dma((chunks, lanes)),
            dma((chunks, lanes)),
            dma((3,)),
            dma((3,)),
            dma,
            dma((5,)),
            dma((chunks,)),
        ],
        compiler_params=pltpu.CompilerParams(
            collective_id=0, has_side_effects=True, vmem_limit_bytes=60 * 2**20
        ),
        cost_estimate=pl.CostEstimate(
            flops=2 * 2 * SLOTS * block * channels * channels,
            bytes_accessed=4 * SLOTS * block * channels * 2,
            transcendentals=0,
        ),
    )(class_counts, tap_windows, fringe_taps, visibilities, flag_mask, filter_panels)


def shards(*arrays):
    visibilities, panels = arrays[0], arrays[6]
    groups, lanes = lax.axis_size("tm"), lax.axis_size("freq")
    block, width = visibilities.shape[2:]
    fits = (
        groups == 4
        and lanes == 4
        and panels.shape[0] == 1
        and arrays[5].shape[0] == block
        and block % 16 == 0
        and width % 128 == 0
    )
    if fits:
        return kernel_shards(groups, lanes, *arrays)
    return plain_shards(*arrays)


def solution(mesh):
    return jax.shard_map(
        shards,
        mesh=mesh,
        in_specs=(
            P(None, "grp", "tm", "freq"),
            P("grp"),
            P("grp"),
            P("grp"),
            P(None, "grp", None),
            P("freq", None),
            P(("grp", "tm"), "freq", None),
        ),
        out_specs=P(None, ("grp", "tm"), None, "freq", None),
        check_vma=False,
    )
```

```python
import functools

import jax
import jax.numpy as jnp
from jax import lax
from jax.experimental import pallas as pl
from jax.experimental.pallas import tpu as pltpu
from jax.sharding import PartitionSpec as P

SLOTS = 32
REACH = 4
SIZES = (8, 8, 4, 4, 4, 2, 2)
STARTS = tuple(sum(SIZES[:k]) for k in range(len(SIZES)))
AHEAD = 16
MESH = pl.DeviceIdType.MESH


def extended(cells, sides, width):
    for axis, dim in sides:
        count = lax.axis_size(axis)
        ends = count - 1
        head = lax.slice_in_dim(cells, 0, width, axis=dim)
        tail = lax.slice_in_dim(cells, cells.shape[dim] - width, cells.shape[dim], axis=dim)
        cells = jnp.concatenate(
            [
                lax.ppermute(tail, axis, [(i, (i + 1) % count) for i in range(ends)]),
                cells,
                lax.ppermute(head, axis, [((i + 1) % count, i) for i in range(ends)]),
            ],
            axis=dim,
        )
    return cells


def masked_taps(fringe_taps, tap_windows):
    offsets = jnp.abs(jnp.arange(2 * REACH + 1, dtype=jnp.int32) - REACH)
    keep = (offsets[None, :] <= tap_windows[:, None]).astype(jnp.float32)
    return fringe_taps * keep[None, :, :]


def convolve(padded, row_taps, length):
    real_part = jnp.zeros(padded.shape[1:2] + (length,) + padded.shape[3:], jnp.float32)
    imag_part = jnp.zeros_like(real_part)
    for offset in range(2 * REACH + 1):
        shifted = lax.slice_in_dim(padded, 2 * REACH - offset, 2 * REACH - offset + length, axis=2)
        tap_real = row_taps[0, :, offset][:, None, None]
        tap_imag = row_taps[1, :, offset][:, None, None]
        real_part = real_part + tap_real * shifted[0] - tap_imag * shifted[1]
        imag_part = imag_part + tap_real * shifted[1] + tap_imag * shifted[0]
    return jnp.stack([real_part, imag_part]).astype(jnp.bfloat16)


def to_slots(per_baseline, class_counts):
    class_starts = jnp.cumsum(class_counts) - class_counts
    slot_positions = jnp.arange(SLOTS, dtype=jnp.int32)
    input_visibility = jnp.clip(
        class_starts[:, None] + slot_positions[None, :], 0, per_baseline.shape[1] - 1
    )
    live_slot = slot_positions[None, :] < class_counts[:, None]
    gathered = jnp.take(per_baseline, input_visibility.reshape(-1), axis=1)
    gathered = gathered.reshape(per_baseline.shape[:1] + live_slot.shape + per_baseline.shape[2:])
    return jnp.where(live_slot[None, :, :, None, None], gathered, jnp.zeros((), per_baseline.dtype))


def plain_shards(
    visibilities, class_ids, class_counts, tap_windows, fringe_taps, flag_mask, filter_panels
):
    taps_kept = masked_taps(fringe_taps, tap_windows)
    padded = extended(visibilities, (("tm", 2),), REACH)
    class_iota = jnp.arange(taps_kept.shape[1], dtype=jnp.int32)
    one_hot = (class_ids[:, None] == class_iota[None, :]).astype(jnp.float32)
    row_taps = jnp.einsum("bc,rck->rbk", one_hot, taps_kept, precision=lax.Precision.HIGHEST)
    filtered = convolve(padded, row_taps, visibilities.shape[2])
    slotted = to_slots(filtered, class_counts)
    local_block = lax.all_to_all(
        lax.all_to_all(slotted, "tm", split_axis=1, concat_axis=3, tiled=True),
        "freq",
        split_axis=3,
        concat_axis=4,
        tiled=True,
    )
    flag_gate = flag_mask.astype(jnp.bfloat16)
    weighted = local_block * flag_gate
    dayenu_fit = jnp.einsum(
        "rcstj,cij->rcsti",
        weighted,
        lax.all_gather(filter_panels, "freq", axis=1, tiled=True),
        preferred_element_type=jnp.float32,
    )
    return (local_block.astype(jnp.float32) - dayenu_fit).astype(jnp.bfloat16)


def tap_matrix(taps_ref, windows_ref, own_class, steps, block):
    size = 2 * steps
    out_pos = lax.broadcasted_iota(jnp.int32, (size, size), 0)
    in_pos = lax.broadcasted_iota(jnp.int32, (size, size), 1)

    def parts(pos):
        return (pos // (2 * block)) * block + pos % block, (pos // block) % 2

    out_t, out_r = parts(out_pos)
    in_t, in_r = parts(in_pos)
    lag = out_t - in_t
    same = out_r == in_r
    sign = (out_r - in_r).astype(jnp.float32)
    matrix = jnp.zeros((size, size), jnp.float32)
    window = windows_ref[own_class]
    for offset in range(2 * REACH + 1):
        keep = jnp.where(abs(offset - REACH) <= window, 1.0, 0.0)
        real = taps_ref[0, own_class, offset] * keep
        imag = taps_ref[1, own_class, offset] * keep
        value = jnp.where(same, real, sign * imag)
        matrix = jnp.where(lag == offset - REACH, value, matrix)
    return matrix


def kernel(
    groups,
    lanes,
    counts_hbm,
    windows_hbm,
    taps_hbm,
    vis_hbm,
    flag_hbm,
    panel_ref,
    out_ref,
    counts_ref,
    windows_ref,
    taps_ref,
    flag_ref,
    vis_ref,
    send_z,
    land_z,
    send_x,
    land_x,
    panels,
    panels_t,
    taps_mat,
    weighted,
    result,
    z_send_sem,
    z_recv_sem,
    x_send_sem,
    x_recv_sem,
    p_send_sem,
    p_recv_sem,
    local_sem,
    fetch_sem,
    out_sem,
):
    my_z = lax.axis_index("tm")
    my_f = lax.axis_index("freq")
    block = vis_ref.shape[2]
    width = vis_ref.shape[3]
    baselines = vis_ref.shape[1]

    def z_peer(d):
        return lax.rem(my_z + d, groups)

    def f_peer(d):
        return lax.rem(my_f + d, lanes)

    core_peer = my_f + 1 - 2 * lax.rem(my_f, 2)
    x_peer = f_peer(2)
    far_peer = core_peer + 2 - 4 * (core_peer // 2)

    fetches = [
        pltpu.make_async_copy(source, target, fetch_sem.at[i])
        for i, (source, target) in enumerate(
            (
                (counts_hbm, counts_ref),
                (vis_hbm, vis_ref),
                (taps_hbm, taps_ref),
                (windows_hbm, windows_ref),
                (flag_hbm, flag_ref),
            )
        )
    ]
    for fetch in fetches:
        fetch.start()

    barrier = pltpu.get_barrier_semaphore()
    for d in range(1, groups):
        pl.semaphore_signal(barrier, inc=1, device_id={"tm": z_peer(d)}, device_id_type=MESH)
    for d in range(1, lanes):
        pl.semaphore_signal(barrier, inc=1, device_id={"freq": f_peer(d)}, device_id_type=MESH)
    pl.semaphore_wait(barrier, groups + lanes - 2)

    def panel_copy(which, source, owner, target):
        return pltpu.make_async_remote_copy(
            src_ref=source,
            dst_ref=panels.at[owner],
            send_sem=p_send_sem.at[which],
            recv_sem=p_recv_sem.at[which],
            device_id={"freq": target},
            device_id_type=MESH,
        )

    to_x = panel_copy(0, panel_ref.at[0], my_f, x_peer)
    to_core = panel_copy(1, panel_ref.at[0], my_f, core_peer)
    own_panel = pltpu.make_async_copy(panel_ref.at[0], panels.at[my_f], local_sem)

    def span(k):
        return pl.ds(STARTS[k], SIZES[k])

    def z_copy(k, target, source):
        return pltpu.make_async_remote_copy(
            src_ref=send_z.at[target, :, span(k)],
            dst_ref=land_z.at[source, :, span(k)],
            send_sem=z_send_sem.at[k, target],
            recv_sem=z_recv_sem.at[k, source],
            device_id={"tm": target},
            device_id_type=MESH,
        )

    def x_copy(k, target, source):
        return pltpu.make_async_remote_copy(
            src_ref=send_x.at[target, :, span(k)],
            dst_ref=land_x.at[source, :, span(k)],
            send_sem=x_send_sem.at[k, target],
            recv_sem=x_recv_sem.at[k, source],
            device_id={"freq": target},
            device_id_type=MESH,
        )

    def pairs(first, count, body):
        def pair(i, carry):
            for u in range(2):
                body(first + 2 * i + u)
            return carry

        lax.fori_loop(0, count // 2, pair, 0)

    def start_of(number):
        total = 0
        for i in range(groups):
            total = total + jnp.where(i < number, counts_ref[i], 0)
        return total

    def pick(number, first, count, target_ref, place):
        class_start = start_of(number)

        def one(slot):
            row = jnp.minimum(class_start + slot, baselines - 1)
            for r in range(2):
                target_ref[place, r, slot] = vis_ref[r, row]

        pairs(first, count, one)

    def send_chunk(k, target):
        pick(target, STARTS[k], SIZES[k], send_z, target)
        z_copy(k, target, my_z).start()

    near = my_z + 1 - 2 * lax.rem(my_z, 2)
    across = (z_peer(2), lax.rem(near + 2, groups))

    def send_all(k):
        send_chunk(k, near)
        for target in across:
            send_chunk(k, target)

    fetches[0].wait()
    fetches[1].wait()
    send_all(0)
    to_x.start()
    to_core.start()
    own_panel.start()
    sent = [k for k in range(len(SIZES)) if STARTS[k] < AHEAD]
    for k in sent[1:]:
        send_all(k)

    for fetch in fetches[2:]:
        fetch.wait()

    pick(my_z, 0, SLOTS, land_z, my_z)

    full = tap_matrix(taps_ref, windows_ref, my_z, groups * block, block)
    size = 2 * groups * block
    high = full.astype(jnp.bfloat16)
    taps_mat[:size, :] = high
    taps_mat[size:, :] = (full - high.astype(jnp.float32)).astype(jnp.bfloat16)
    live_count = counts_ref[my_z]

    def filter_chunk(k):
        for d in range(1, groups):
            z_copy(k, my_z, z_peer(d)).wait_recv()

        def one(slot):
            cells = land_z[:, :, slot].reshape(size, width)
            both = jnp.dot(taps_mat[...], cells, preferred_element_type=jnp.float32)
            live = jnp.where(slot < live_count, 1.0, 0.0)
            filtered = (both[:size] + both[size:]) * live
            send_x[:, :, slot] = filtered.astype(jnp.bfloat16).reshape(lanes, 2, block, width)

        pairs(STARTS[k], SIZES[k], one)
        for d in (2, 1, 3):
            x_copy(k, f_peer(d), my_f).start()
        land_x[my_f, :, span(k)] = send_x[my_f, :, span(k)]
        for later in range(len(SIZES)):
            if later not in sent and STARTS[later] < STARTS[k] + SIZES[k] + AHEAD:
                send_all(later)
                sent.append(later)

    def out_copy(k):
        return pltpu.make_async_copy(
            result.at[:, span(k)], out_ref.at[:, 0, span(k)], out_sem.at[k]
        )

    def fit_chunk(k):
        count = SIZES[k]
        rows = 2 * count * block
        for d in range(1, lanes):
            x_copy(k, my_f, f_peer(d)).wait_recv()
        for j in range(lanes):
            gate = flag_ref[:, j * width : (j + 1) * width].astype(jnp.bfloat16)
            weighted[:rows, j * width : (j + 1) * width] = (
                land_x[j, :, span(k)] * gate
            ).reshape(rows, width)

        def one_block(i, carry):
            fit = jnp.dot(weighted[:rows], panels_t[i], preferred_element_type=jnp.float32)
            columns = pl.ds(pl.multiple_of(i * width, width), width)
            slotted = land_x[i, :, span(k)].astype(jnp.float32).reshape(rows, width)
            cleaned = (slotted - fit).astype(jnp.bfloat16)
            result[:, span(k), :, columns] = cleaned.reshape(2, count, block, width)
            return carry

        lax.fori_loop(0, lanes, one_block, 0)
        out_copy(k).start()

    def turn(i):
        panels_t[i] = panels[i].T

    own_panel.wait()
    turn(my_f)
    filter_chunk(0)
    panel_copy(1, panel_ref.at[0], core_peer, my_f).wait_recv()
    turn(core_peer)
    filter_chunk(1)
    panel_copy(0, panel_ref.at[0], x_peer, my_f).wait_recv()
    forward = panel_copy(2, panels.at[x_peer], x_peer, core_peer)
    forward.start()
    turn(x_peer)
    filter_chunk(2)
    panel_copy(2, panel_ref.at[0], far_peer, my_f).wait_recv()
    turn(far_peer)
    last = len(SIZES) - 1
    fit_chunk(0)
    for k in range(3, last):
        filter_chunk(k)
        fit_chunk(k - 2)
    fit_chunk(last - 2)
    filter_chunk(last)
    fit_chunk(last - 1)
    fit_chunk(last)

    for k in range(len(SIZES)):
        out_copy(k).wait()
        for d in range(1, groups):
            z_copy(k, z_peer(d), my_z).wait_send()
        for d in range(1, lanes):
            x_copy(k, f_peer(d), my_f).wait_send()
    to_x.wait_send()
    to_core.wait_send()
    forward.wait_send()


def kernel_shards(
    groups, lanes, visibilities, class_ids, class_counts, tap_windows, fringe_taps, flag_mask, filter_panels
):
    block, width = visibilities.shape[2:]
    channels = lanes * width
    chunks = len(SIZES)
    size = 2 * groups * block
    bf16 = jnp.bfloat16
    hbm = pl.BlockSpec(memory_space=pltpu.HBM)
    dma = pltpu.SemaphoreType.DMA
    return pl.pallas_call(
        functools.partial(kernel, groups, lanes),
        out_shape=jax.ShapeDtypeStruct((2, 1, SLOTS, block, channels), bf16),
        in_specs=[hbm] * 6,
        out_specs=pl.BlockSpec(memory_space=pl.ANY),
        scratch_shapes=[
            pltpu.SMEM(class_counts.shape, jnp.int32),
            pltpu.SMEM(tap_windows.shape, jnp.int32),
            pltpu.SMEM(fringe_taps.shape, jnp.float32),
            pltpu.VMEM(flag_mask.shape, jnp.int32),
            pltpu.VMEM(visibilities.shape, bf16),
            pltpu.VMEM((groups, 2, SLOTS, block, width), bf16),
            pltpu.VMEM((groups, 2, SLOTS, block, width), bf16),
            pltpu.VMEM((lanes, 2, SLOTS, block, width), bf16),
            pltpu.VMEM((lanes, 2, SLOTS, block, width), bf16),
            pltpu.VMEM((lanes, width, channels), bf16),
            pltpu.VMEM((lanes, channels, width), bf16),
            pltpu.VMEM((2 * size, size), bf16),
            pltpu.VMEM((2 * max(SIZES) * block, channels), bf16),
            pltpu.VMEM((2, SLOTS, block, channels), bf16),
            dma((chunks, groups)),
            dma((chunks, groups)),
            dma((chunks, lanes)),
            dma((chunks, lanes)),
            dma((3,)),
            dma((3,)),
            dma,
            dma((5,)),
            dma((chunks,)),
        ],
        compiler_params=pltpu.CompilerParams(
            collective_id=0, has_side_effects=True, vmem_limit_bytes=60 * 2**20
        ),
        cost_estimate=pl.CostEstimate(
            flops=2 * 2 * SLOTS * block * channels * channels,
            bytes_accessed=4 * SLOTS * block * channels * 2,
            transcendentals=0,
        ),
    )(class_counts, tap_windows, fringe_taps, visibilities, flag_mask, filter_panels)


def shards(*arrays):
    visibilities, panels = arrays[0], arrays[6]
    groups, lanes = lax.axis_size("tm"), lax.axis_size("freq")
    block, width = visibilities.shape[2:]
    fits = (
        groups == 4
        and lanes == 4
        and panels.shape[0] == 1
        and arrays[5].shape[0] == block
        and block % 16 == 0
        and width % 128 == 0
    )
    if fits:
        return kernel_shards(groups, lanes, *arrays)
    return plain_shards(*arrays)


def solution(mesh):
    return jax.shard_map(
        shards,
        mesh=mesh,
        in_specs=(
            P(None, "grp", "tm", "freq"),
            P("grp"),
            P("grp"),
            P("grp"),
            P(None, "grp", None),
            P("freq", None),
            P(("grp", "tm"), "freq", None),
        ),
        out_specs=P(None, ("grp", "tm"), None, "freq", None),
        check_vma=False,
    )
```

```python
import functools

import jax
import jax.numpy as jnp
from jax import lax
from jax.experimental import pallas as pl
from jax.experimental.pallas import tpu as pltpu
from jax.sharding import PartitionSpec as P

SLOTS = 32
REACH = 4
SIZES = (8, 8, 8, 4, 4)
STARTS = tuple(sum(SIZES[:k]) for k in range(len(SIZES)))
AHEAD = 16
MESH = pl.DeviceIdType.MESH


def extended(cells, sides, width):
    for axis, dim in sides:
        count = lax.axis_size(axis)
        ends = count - 1
        head = lax.slice_in_dim(cells, 0, width, axis=dim)
        tail = lax.slice_in_dim(cells, cells.shape[dim] - width, cells.shape[dim], axis=dim)
        cells = jnp.concatenate(
            [
                lax.ppermute(tail, axis, [(i, (i + 1) % count) for i in range(ends)]),
                cells,
                lax.ppermute(head, axis, [((i + 1) % count, i) for i in range(ends)]),
            ],
            axis=dim,
        )
    return cells


def masked_taps(fringe_taps, tap_windows):
    offsets = jnp.abs(jnp.arange(2 * REACH + 1, dtype=jnp.int32) - REACH)
    keep = (offsets[None, :] <= tap_windows[:, None]).astype(jnp.float32)
    return fringe_taps * keep[None, :, :]


def convolve(padded, row_taps, length):
    real_part = jnp.zeros(padded.shape[1:2] + (length,) + padded.shape[3:], jnp.float32)
    imag_part = jnp.zeros_like(real_part)
    for offset in range(2 * REACH + 1):
        shifted = lax.slice_in_dim(padded, 2 * REACH - offset, 2 * REACH - offset + length, axis=2)
        tap_real = row_taps[0, :, offset][:, None, None]
        tap_imag = row_taps[1, :, offset][:, None, None]
        real_part = real_part + tap_real * shifted[0] - tap_imag * shifted[1]
        imag_part = imag_part + tap_real * shifted[1] + tap_imag * shifted[0]
    return jnp.stack([real_part, imag_part]).astype(jnp.bfloat16)


def to_slots(per_baseline, class_counts):
    class_starts = jnp.cumsum(class_counts) - class_counts
    slot_positions = jnp.arange(SLOTS, dtype=jnp.int32)
    input_visibility = jnp.clip(
        class_starts[:, None] + slot_positions[None, :], 0, per_baseline.shape[1] - 1
    )
    live_slot = slot_positions[None, :] < class_counts[:, None]
    gathered = jnp.take(per_baseline, input_visibility.reshape(-1), axis=1)
    gathered = gathered.reshape(per_baseline.shape[:1] + live_slot.shape + per_baseline.shape[2:])
    return jnp.where(live_slot[None, :, :, None, None], gathered, jnp.zeros((), per_baseline.dtype))


def plain_shards(
    visibilities, class_ids, class_counts, tap_windows, fringe_taps, flag_mask, filter_panels
):
    taps_kept = masked_taps(fringe_taps, tap_windows)
    padded = extended(visibilities, (("tm", 2),), REACH)
    class_iota = jnp.arange(taps_kept.shape[1], dtype=jnp.int32)
    one_hot = (class_ids[:, None] == class_iota[None, :]).astype(jnp.float32)
    row_taps = jnp.einsum("bc,rck->rbk", one_hot, taps_kept, precision=lax.Precision.HIGHEST)
    filtered = convolve(padded, row_taps, visibilities.shape[2])
    slotted = to_slots(filtered, class_counts)
    local_block = lax.all_to_all(
        lax.all_to_all(slotted, "tm", split_axis=1, concat_axis=3, tiled=True),
        "freq",
        split_axis=3,
        concat_axis=4,
        tiled=True,
    )
    flag_gate = flag_mask.astype(jnp.bfloat16)
    weighted = local_block * flag_gate
    dayenu_fit = jnp.einsum(
        "rcstj,cij->rcsti",
        weighted,
        lax.all_gather(filter_panels, "freq", axis=1, tiled=True),
        preferred_element_type=jnp.float32,
    )
    return (local_block.astype(jnp.float32) - dayenu_fit).astype(jnp.bfloat16)


def tap_matrix(taps_ref, windows_ref, own_class, steps):
    size = 2 * steps
    out_pos = lax.broadcasted_iota(jnp.int32, (size, size), 0)
    in_pos = lax.broadcasted_iota(jnp.int32, (size, size), 1)

    def parts(pos):
        return pos % steps, pos // steps

    out_t, out_r = parts(out_pos)
    in_t, in_r = parts(in_pos)
    lag = out_t - in_t
    same = out_r == in_r
    sign = (out_r - in_r).astype(jnp.float32)
    matrix = jnp.zeros((size, size), jnp.float32)
    window = windows_ref[own_class]
    for offset in range(2 * REACH + 1):
        keep = jnp.where(abs(offset - REACH) <= window, 1.0, 0.0)
        real = taps_ref[0, own_class, offset] * keep
        imag = taps_ref[1, own_class, offset] * keep
        value = jnp.where(same, real, sign * imag)
        matrix = jnp.where(lag == offset - REACH, value, matrix)
    return matrix


def kernel(
    groups,
    lanes,
    counts_hbm,
    windows_hbm,
    taps_hbm,
    vis_hbm,
    flag_hbm,
    panel_ref,
    out_ref,
    counts_ref,
    windows_ref,
    taps_ref,
    flag_ref,
    vis_ref,
    send_z,
    land_z,
    send_x,
    land_x,
    panels,
    panels_t,
    taps_mat,
    weighted,
    result,
    z_send_sem,
    z_recv_sem,
    x_send_sem,
    x_recv_sem,
    p_send_sem,
    p_recv_sem,
    local_sem,
    fetch_sem,
    out_sem,
):
    my_z = lax.axis_index("tm")
    my_f = lax.axis_index("freq")
    block = vis_ref.shape[2]
    width = vis_ref.shape[3]
    baselines = vis_ref.shape[1]

    def z_peer(d):
        return lax.rem(my_z + d, groups)

    def f_peer(d):
        return lax.rem(my_f + d, lanes)

    core_peer = my_f + 1 - 2 * lax.rem(my_f, 2)
    x_peer = f_peer(2)
    far_peer = core_peer + 2 - 4 * (core_peer // 2)

    fetches = [
        pltpu.make_async_copy(source, target, fetch_sem.at[i])
        for i, (source, target) in enumerate(
            (
                (counts_hbm, counts_ref),
                (vis_hbm, vis_ref),
                (taps_hbm, taps_ref),
                (windows_hbm, windows_ref),
                (flag_hbm, flag_ref),
            )
        )
    ]
    for fetch in fetches:
        fetch.start()

    barrier = pltpu.get_barrier_semaphore()
    for d in range(1, groups):
        pl.semaphore_signal(barrier, inc=1, device_id={"tm": z_peer(d)}, device_id_type=MESH)
    for d in range(1, lanes):
        pl.semaphore_signal(barrier, inc=1, device_id={"freq": f_peer(d)}, device_id_type=MESH)
    pl.semaphore_wait(barrier, groups + lanes - 2)

    def panel_copy(which, source, owner, target):
        return pltpu.make_async_remote_copy(
            src_ref=source,
            dst_ref=panels.at[owner],
            send_sem=p_send_sem.at[which],
            recv_sem=p_recv_sem.at[which],
            device_id={"freq": target},
            device_id_type=MESH,
        )

    to_x = panel_copy(0, panel_ref.at[0], my_f, x_peer)
    to_core = panel_copy(1, panel_ref.at[0], my_f, core_peer)
    own_panel = pltpu.make_async_copy(panel_ref.at[0], panels.at[my_f], local_sem)

    def span(k):
        return pl.ds(STARTS[k], SIZES[k])

    def both_spans(k):
        return pl.ds(2 * STARTS[k], 2 * SIZES[k])

    def place_of(k, r, slot):
        return STARTS[k] + r * SIZES[k] + slot

    def z_copy(k, target, source):
        return pltpu.make_async_remote_copy(
            src_ref=send_z.at[target, both_spans(k)],
            dst_ref=land_z.at[source, both_spans(k)],
            send_sem=z_send_sem.at[k, target],
            recv_sem=z_recv_sem.at[k, source],
            device_id={"tm": target},
            device_id_type=MESH,
        )

    def x_copy(k, target, source):
        return pltpu.make_async_remote_copy(
            src_ref=send_x.at[target, both_spans(k)],
            dst_ref=land_x.at[source, both_spans(k)],
            send_sem=x_send_sem.at[k, target],
            recv_sem=x_recv_sem.at[k, source],
            device_id={"freq": target},
            device_id_type=MESH,
        )

    def pairs(first, count, body):
        def pair(i, carry):
            for u in range(2):
                body(first + 2 * i + u)
            return carry

        lax.fori_loop(0, count // 2, pair, 0)

    def start_of(number):
        total = 0
        for i in range(groups):
            total = total + jnp.where(i < number, counts_ref[i], 0)
        return total

    def pick(number, k, target_ref):
        class_start = start_of(number)

        def one(slot):
            row = jnp.minimum(class_start + slot, baselines - 1)
            for r in range(2):
                target_ref[number, place_of(k, r, slot)] = vis_ref[r, row]

        pairs(STARTS[k], SIZES[k], one)

    def send_chunk(k, target):
        pick(target, k, send_z)
        z_copy(k, target, my_z).start()

    near = my_z + 1 - 2 * lax.rem(my_z, 2)
    across = (z_peer(2), lax.rem(near + 2, groups))

    def send_all(k):
        send_chunk(k, near)
        for target in across:
            send_chunk(k, target)

    fetches[0].wait()
    fetches[1].wait()
    send_all(0)
    to_x.start()
    to_core.start()
    own_panel.start()
    sent = [k for k in range(len(SIZES)) if STARTS[k] < AHEAD]
    for k in sent[1:]:
        send_all(k)

    for fetch in fetches[2:]:
        fetch.wait()

    for k in range(len(SIZES)):
        pick(my_z, k, land_z)

    steps = groups * block
    full = tap_matrix(taps_ref, windows_ref, my_z, steps)
    size = 2 * steps
    high = full.astype(jnp.bfloat16)
    taps_mat[:size, :] = high
    taps_mat[size:, :] = (full - high.astype(jnp.float32)).astype(jnp.bfloat16)
    live_count = counts_ref[my_z]

    def filter_chunk(k):
        for d in range(1, groups):
            z_copy(k, my_z, z_peer(d)).wait_recv()

        def one(slot):
            cells = jnp.concatenate(
                [land_z[:, place_of(k, r, slot)].reshape(steps, width) for r in range(2)]
            )
            both = jnp.dot(taps_mat[...], cells, preferred_element_type=jnp.float32)
            live = jnp.where(slot < live_count, 1.0, 0.0)
            filtered = (both[:size] + both[size:]) * live
            filtered = filtered.astype(jnp.bfloat16)
            for r in range(2):
                part = filtered[r * steps : (r + 1) * steps]
                send_x[:, place_of(k, r, slot)] = part.reshape(lanes, block, width)

        pairs(STARTS[k], SIZES[k], one)
        for d in (2, 1, 3):
            x_copy(k, f_peer(d), my_f).start()
        land_x[my_f, both_spans(k)] = send_x[my_f, both_spans(k)]
        for later in range(len(SIZES)):
            if later not in sent and STARTS[later] < STARTS[k] + SIZES[k] + AHEAD:
                send_all(later)
                sent.append(later)

    def out_copy(k):
        return pltpu.make_async_copy(
            result.at[:, span(k)], out_ref.at[:, 0, span(k)], out_sem.at[k]
        )

    def fit_chunk(k):
        count = SIZES[k]
        rows = 2 * count * block
        for d in range(1, lanes):
            x_copy(k, my_f, f_peer(d)).wait_recv()
        for j in range(lanes):
            gate = flag_ref[:, j * width : (j + 1) * width].astype(jnp.bfloat16)
            weighted[:rows, j * width : (j + 1) * width] = (
                land_x[j, both_spans(k)] * gate
            ).reshape(rows, width)

        def one_block(i, carry):
            fit = jnp.dot(weighted[:rows], panels_t[i], preferred_element_type=jnp.float32)
            columns = pl.ds(pl.multiple_of(i * width, width), width)
            slotted = land_x[i, both_spans(k)].astype(jnp.float32).reshape(rows, width)
            cleaned = (slotted - fit).astype(jnp.bfloat16)
            result[:, span(k), :, columns] = cleaned.reshape(2, count, block, width)
            return carry

        lax.fori_loop(0, lanes, one_block, 0)
        out_copy(k).start()

    def turn(i):
        panels_t[i] = panels[i].T

    own_panel.wait()
    turn(my_f)
    filter_chunk(0)
    panel_copy(1, panel_ref.at[0], core_peer, my_f).wait_recv()
    turn(core_peer)
    filter_chunk(1)
    panel_copy(0, panel_ref.at[0], x_peer, my_f).wait_recv()
    forward = panel_copy(2, panels.at[x_peer], x_peer, core_peer)
    forward.start()
    turn(x_peer)
    filter_chunk(2)
    panel_copy(2, panel_ref.at[0], far_peer, my_f).wait_recv()
    turn(far_peer)
    last = len(SIZES) - 1
    fit_chunk(0)
    for k in range(3, last):
        filter_chunk(k)
        fit_chunk(k - 2)
    fit_chunk(last - 2)
    filter_chunk(last)
    fit_chunk(last - 1)
    fit_chunk(last)

    for k in range(len(SIZES)):
        out_copy(k).wait()
        for d in range(1, groups):
            z_copy(k, z_peer(d), my_z).wait_send()
        for d in range(1, lanes):
            x_copy(k, f_peer(d), my_f).wait_send()
    to_x.wait_send()
    to_core.wait_send()
    forward.wait_send()


def kernel_shards(
    groups, lanes, visibilities, class_ids, class_counts, tap_windows, fringe_taps, flag_mask, filter_panels
):
    block, width = visibilities.shape[2:]
    channels = lanes * width
    chunks = len(SIZES)
    size = 2 * groups * block
    bf16 = jnp.bfloat16
    hbm = pl.BlockSpec(memory_space=pltpu.HBM)
    dma = pltpu.SemaphoreType.DMA
    return pl.pallas_call(
        functools.partial(kernel, groups, lanes),
        out_shape=jax.ShapeDtypeStruct((2, 1, SLOTS, block, channels), bf16),
        in_specs=[hbm] * 6,
        out_specs=pl.BlockSpec(memory_space=pl.ANY),
        scratch_shapes=[
            pltpu.SMEM(class_counts.shape, jnp.int32),
            pltpu.SMEM(tap_windows.shape, jnp.int32),
            pltpu.SMEM(fringe_taps.shape, jnp.float32),
            pltpu.VMEM(flag_mask.shape, jnp.int32),
            pltpu.VMEM(visibilities.shape, bf16),
            pltpu.VMEM((groups, 2 * SLOTS, block, width), bf16),
            pltpu.VMEM((groups, 2 * SLOTS, block, width), bf16),
            pltpu.VMEM((lanes, 2 * SLOTS, block, width), bf16),
            pltpu.VMEM((lanes, 2 * SLOTS, block, width), bf16),
            pltpu.VMEM((lanes, width, channels), bf16),
            pltpu.VMEM((lanes, channels, width), bf16),
            pltpu.VMEM((2 * size, size), bf16),
            pltpu.VMEM((2 * max(SIZES) * block, channels), bf16),
            pltpu.VMEM((2, SLOTS, block, channels), bf16),
            dma((chunks, groups)),
            dma((chunks, groups)),
            dma((chunks, lanes)),
            dma((chunks, lanes)),
            dma((3,)),
            dma((3,)),
            dma,
            dma((5,)),
            dma((chunks,)),
        ],
        compiler_params=pltpu.CompilerParams(
            collective_id=0, has_side_effects=True, vmem_limit_bytes=60 * 2**20
        ),
        cost_estimate=pl.CostEstimate(
            flops=2 * 2 * SLOTS * block * channels * channels,
            bytes_accessed=4 * SLOTS * block * channels * 2,
            transcendentals=0,
        ),
    )(class_counts, tap_windows, fringe_taps, visibilities, flag_mask, filter_panels)


def shards(*arrays):
    visibilities, panels = arrays[0], arrays[6]
    groups, lanes = lax.axis_size("tm"), lax.axis_size("freq")
    block, width = visibilities.shape[2:]
    fits = (
        groups == 4
        and lanes == 4
        and panels.shape[0] == 1
        and arrays[5].shape[0] == block
        and block % 16 == 0
        and width % 128 == 0
    )
    if fits:
        return kernel_shards(groups, lanes, *arrays)
    return plain_shards(*arrays)


def solution(mesh):
    return jax.shard_map(
        shards,
        mesh=mesh,
        in_specs=(
            P(None, "grp", "tm", "freq"),
            P("grp"),
            P("grp"),
            P("grp"),
            P(None, "grp", None),
            P("freq", None),
            P(("grp", "tm"), "freq", None),
        ),
        out_specs=P(None, ("grp", "tm"), None, "freq", None),
        check_vma=False,
    )
```
